256 devices in a mesh: seq: 32 (over z, x), head: 8 (over y, core).
Axes of the slice: x: 4, y: 4, z: 8, core: 2. Of those that a mesh axis runs over, the one named last changes fastest.
Arguments:
- query_states: bfloat16 [12288, 5120], P('seq', 'head')
- key_states: bfloat16 [12288, 5120], P('seq', 'head')
- value_states: bfloat16 [12288, 5120], P('seq', 'head')
- gate_states: bfloat16 [12288, 5120], P('seq', 'head'), may hold values from -8 to 8
- selection: int32 [192, 32], P('seq'), may hold values from 0 to 191, as said below
- out_weight: bfloat16 [5120, 5120], P('head'), may hold values from -0.078125 to 0.078125
Outputs:
- projected: bfloat16 [12288, 5120], P(('seq', 'head'))
The draws below stay inside these ranges and needn't reach their ends.
Inputs may be any that keep to these rules, and one draw needn't show every extreme that they name: `selection`: each row names 32 different cubes. Taken together, the rows of one index of seq (aligned blocks of 6 rows) name at most 4 different cubes among the 6 cubes of any one index of seq, and exactly 4 of some index.
All inputs are finite; a program needn't handle non-finite values.
Results may differ from the reference program's by a relative error of at most 0.02.
Values may be sent and summed in bfloat16 or wider, within the bound.
A program may use at most 256 MiB of HBM per device.

```python
import jax
import jax.numpy as jnp
from jax import lax

D = 5120
HEAD_DIM = 128
HEADS = 40
CUBE = 64
TOPK = 32
CAP = 4
CUBE_DEV = 6
NCUBES = 192
TOKENS = 12288
N_SEQ = 32


def cube_base(key):
    return jax.random.normal(jax.random.fold_in(key, 7), (NCUBES, HEADS * HEAD_DIM), jnp.float32)


def selection_lists(key):
    key = jax.random.fold_in(key, 21)
    subkeys = jax.random.split(key, 5)
    owner_count = N_SEQ
    need_owners = (TOPK + CAP - 1) // CAP
    owner_rank = jax.vmap(lambda item: jax.random.permutation(item, owner_count))(jax.random.split(subkeys[0], owner_count))
    chosen_owner = jax.random.randint(subkeys[1], (), 0, owner_count)
    full_owner = (owner_rank < need_owners) | (jnp.arange(owner_count)[None, :] == chosen_owner)
    counts = jnp.where(full_owner, CAP, jax.random.randint(subkeys[2], (owner_count, owner_count), 0, CAP + 1))
    order = jax.vmap(lambda item: jax.random.permutation(item, CUBE_DEV))(jax.random.split(subkeys[3], owner_count * owner_count))
    order = order.reshape(owner_count, owner_count, CUBE_DEV)
    candidate = (order < counts[:, :, None]).reshape(owner_count, NCUBES)
    raw_scores = jax.random.randint(subkeys[4], (NCUBES, NCUBES), 0, 2 ** 18)
    columns = jnp.arange(NCUBES, dtype=jnp.int32)
    row_device = columns // CUBE_DEV
    row_candidate = candidate[row_device]
    first_row = (columns % CUBE_DEV == 0)[:, None]
    boosted = first_row & (columns // CUBE_DEV == chosen_owner)[None, :]
    scores = raw_scores * NCUBES + columns[None, :] + 1 + jnp.where(boosted, 2 ** 29, 0)
    scores = jnp.where(row_candidate, scores, 0)
    picked = lax.top_k(scores, TOPK)[1]
    return picked.astype(jnp.int32)


def draw_selection(key, part):
    return selection_lists(key)


def draw_key_states(key, part):
    common = cube_base(key)
    key = jax.random.fold_in(key, 1)
    noise = jax.random.normal(key, (TOKENS, HEADS * HEAD_DIM), jnp.float32)
    result = 0.8 * jnp.repeat(common, CUBE, axis=0) + 0.6 * noise
    return result.astype(jnp.bfloat16)


def draw_value_states(key, part):
    key = jax.random.fold_in(key, 2)
    split_keys = jax.random.split(key, 2)
    common = jax.random.normal(split_keys[0], (NCUBES, HEADS * HEAD_DIM), jnp.float32)
    noise = jax.random.normal(split_keys[1], (TOKENS, HEADS * HEAD_DIM), jnp.float32)
    result = 0.7 * jnp.repeat(common, CUBE, axis=0) + 0.7 * noise
    return result.astype(jnp.bfloat16)


def draw_query_states(key, part):
    key = jax.random.fold_in(key, 4)
    split_keys = jax.random.split(key, 1)
    result = 2.0 * jax.random.normal(split_keys[0], (TOKENS, HEADS * HEAD_DIM), jnp.float32)
    return result.astype(jnp.bfloat16)


def level_of(rng, dims, cuts, smallest, largest):
    loudness = 1.0
    for dim, shards_of in cuts:
        draws = jax.random.uniform(jax.random.fold_in(jax.random.fold_in(rng, 6), dim), (shards_of,), jnp.float32, smallest / len(cuts), largest / len(cuts))
        loudness = loudness * jnp.repeat(jnp.exp(draws), dims[dim] // shards_of).reshape((-1,) + (1,) * (len(dims) - 1 - dim))
    return loudness


def centred(key, extent, width, bound, pieces=(), held_as=jnp.bfloat16):
    factor_of = level_of(key, extent, pieces, -0.22, 0.18) if pieces else 1.0
    values = jax.random.normal(key, extent, jnp.float32) * width * factor_of
    return jnp.minimum(jnp.maximum(values, -bound), bound).astype(held_as)


def setup_inputs(seed: int = 0) -> dict:
    key_list = jax.random.split(jax.random.key(seed), 7)
    return {
        "query_states": draw_query_states(jax.random.fold_in(key_list[6], 71), 0),
        "key_states": draw_key_states(jax.random.fold_in(key_list[6], 71), 0),
        "value_states": draw_value_states(jax.random.fold_in(key_list[6], 71), 0),
        "gate_states": centred(key_list[3], (TOKENS, HEADS * HEAD_DIM), 1.5, 8.0, ((0, 32), (1, 8))),
        "selection": draw_selection(jax.random.fold_in(key_list[6], 71), 0),
        "out_weight": centred(key_list[5], (HEADS * HEAD_DIM, D), (HEADS * HEAD_DIM) ** -0.5, 0.078125, ((0, 8),)),
    }


def soft_weights(scores):
    top = jnp.max(scores, axis=-1, keepdims=True)
    expo = jnp.exp(scores - top)
    return (expo / jnp.sum(expo, axis=-1, keepdims=True)).astype(jnp.bfloat16)


def reference(query_states, key_states, value_states, gate_states, selection, out_weight):
    feat_width = HEADS * HEAD_DIM
    score_scale = HEAD_DIM ** -0.5
    key_cubes = key_states.reshape(NCUBES, CUBE, HEADS, HEAD_DIM)
    value_cubes = value_states.reshape(NCUBES, CUBE, HEADS, HEAD_DIM)
    pooled_key = jnp.mean(key_cubes.astype(jnp.float32), axis=1).astype(jnp.bfloat16).astype(jnp.float32)
    pooled_value = jnp.mean(value_cubes.astype(jnp.float32), axis=1).astype(jnp.bfloat16).astype(jnp.float32)

    def per_cube(cube_id):
        start = cube_id * CUBE
        queries = lax.dynamic_slice_in_dim(query_states, start, CUBE, 0).astype(jnp.float32).reshape(CUBE, HEADS, HEAD_DIM)
        gates = lax.dynamic_slice_in_dim(gate_states, start, CUBE, 0).astype(jnp.float32).reshape(CUBE, HEADS, HEAD_DIM)
        coarse_scores = jnp.einsum("qhd,khd->hqk", queries, pooled_key) * score_scale
        coarse_weight = soft_weights(coarse_scores).astype(jnp.float32)
        coarse_out = jnp.einsum("hqk,khd->qhd", coarse_weight, pooled_value)
        chosen = lax.dynamic_index_in_dim(selection, cube_id, 0, keepdims=False)
        fine_keys = key_cubes[chosen].reshape(TOPK * CUBE, HEADS, HEAD_DIM).astype(jnp.float32)
        fine_values = value_cubes[chosen].reshape(TOPK * CUBE, HEADS, HEAD_DIM).astype(jnp.float32)
        fine_scores = jnp.einsum("qhd,khd->hqk", queries, fine_keys) * score_scale
        fine_weight = soft_weights(fine_scores).astype(jnp.float32)
        fine_out = jnp.einsum("hqk,khd->qhd", fine_weight, fine_values)
        mixed = jax.nn.sigmoid(gates) * (coarse_out + fine_out)
        return mixed.reshape(CUBE, feat_width).astype(jnp.bfloat16)

    attended = lax.map(per_cube, jnp.arange(NCUBES, dtype=jnp.int32)).reshape(TOKENS, feat_width)
    return jnp.dot(attended, out_weight, preferred_element_type=jnp.float32).astype(jnp.bfloat16)
```

```python
import functools
import math

import jax
import jax.numpy as jnp
from jax import lax
from jax.experimental import pallas as pl
from jax.experimental.pallas import tpu as pltpu
from jax.sharding import PartitionSpec as P

MESH = pl.DeviceIdType.MESH
HEAD_DIM = 128
CUBE = 64
CUBE_DEV = 6
TOPK = 32
NZ, NX = 8, 4
ROWS = CUBE * CUBE_DEV
HEADS_DEV = 5
ORDER = (0, 1, 7, 2, 6, 3, 5, 4)
XORDER = (1, 3, 2)
EXP_SCALE = HEAD_DIM ** (-0.5) * math.log2(math.e)


def place():
    seq, head = lax.axis_index("seq"), lax.axis_index("head")
    return seq // NX, seq % NX, head // 2, head % 2


def remote(src, dst, send_sem, recv_sem, seq, head):
    return pltpu.make_async_remote_copy(
        src_ref=src,
        dst_ref=dst,
        send_sem=send_sem,
        recv_sem=recv_sem,
        device_id={"seq": seq, "head": head},
        device_id_type=MESH,
    )


def arrived(ref, sem):
    pltpu.make_async_copy(ref, ref, sem).wait()


def greet(z, x, y, c):
    barrier = pltpu.get_barrier_semaphore()
    for dz in range(NZ):
        for dc in range(2):
            if dz or dc:
                pl.semaphore_signal(
                    barrier,
                    inc=1,
                    device_id={"seq": (z + dz) % NZ * NX + x, "head": 2 * y + (c + dc) % 2},
                    device_id_type=MESH,
                )
    for dx in range(1, NX):
        pl.semaphore_signal(
            barrier,
            inc=1,
            device_id={"seq": z * NX + (x + dx) % NX, "head": 2 * y + c},
            device_id_type=MESH,
        )
    pl.semaphore_wait(barrier, 2 * NZ - 1 + NX - 1)


def spread_kernel(
    q_ref, k_ref, v_ref, kv_ref, qf_ref, qr_ref,
    z_send, z_recv, x_send, x_recv, xq_send, xq_recv, c_send, c_recv,
):
    z, x, y, c = place()
    here = z * NX + x
    sibling = 2 * y + 1 - c
    main_slot = x + x // 3
    extra_slot = 4 - x // 3
    has_extra = z % 4 != 3
    member = (x != 3) | has_extra
    greet(z, x, y, c)

    def z_copies(act):
        for n, dz in enumerate(ORDER):
            zt = (z + dz) % NZ
            for cc in range(2):
                source = k_ref if cc == 0 else v_ref

                def one(cond, kind, src, dst):
                    def away():
                        copy = remote(
                            src, dst, z_send.at[n, cc, kind], z_recv.at[z, kind], zt * NX + x, 2 * y + cc
                        )
                        if act == "start":
                            copy.start()
                        else:
                            copy.wait_send()

                    if dz:
                        pl.when(cond)(away)
                    else:
                        pl.when(cond & (c != cc))(away)
                        if act == "start":
                            pl.when(cond & (c == cc))(
                                lambda: pltpu.make_async_copy(src, dst, z_recv.at[z, kind]).start()
                            )

                is_main = c == zt // 5
                col = pl.ds(pl.multiple_of(zt % 5 * HEAD_DIM, HEAD_DIM), HEAD_DIM)
                one(is_main, 0, source.at[:, col], kv_ref.at[cc, main_slot, z])
                is_extra = (c == 1) & (zt % 4 != 3)
                xcol = pl.ds(pl.multiple_of((3 + zt // 4) * HEAD_DIM, HEAD_DIM), HEAD_DIM)
                one(is_extra, 1, source.at[:, xcol], kv_ref.at[cc, extra_slot, z])
                one(is_main, 2, q_ref.at[:, cc, :, col], qr_ref.at[pl.ds(0, 3), z])
                rank = zt % 4 - zt % 4 // 3
                one(is_extra, 3, q_ref.at[rank, cc, :, xcol], qr_ref.at[3, z])

    z_copies("start")

    def x_copies(n, zs, act):
        for dx in XORDER:
            xt = (x + dx) % NX
            slot = main_slot + xt // 3 * (4 - main_slot)

            def away():
                copy = remote(
                    kv_ref.at[c, slot, zs], kv_ref.at[c, x, zs],
                    x_send.at[dx, n], x_recv.at[x, zs], z * NX + xt, 2 * y + c,
                )
                if act == "start":
                    copy.start()
                else:
                    copy.wait_send()

            pl.when((xt != 3) | has_extra)(away)

    def core_copy(xs, zs):
        return remote(
            kv_ref.at[c, xs, zs], kv_ref.at[c, xs, zs],
            c_send.at[xs, zs], c_recv.at[xs, zs], here, sibling,
        )

    def take_x(zs):
        for dx in XORDER:
            xs = (x + dx) % NX

            @pl.when(member)
            def _():
                arrived(kv_ref.at[c, xs, zs], x_recv.at[xs, zs])
                core_copy(xs, zs).start()

    lag = 2
    for n, dz in enumerate(ORDER):
        zs = (z + dz) % NZ
        arrived(kv_ref.at[c, main_slot, zs], z_recv.at[zs, 0])
        pl.when(has_extra)(lambda: arrived(kv_ref.at[c, extra_slot, zs], z_recv.at[zs, 1]))
        x_copies(n, zs, "start")
        pl.when(member)(lambda: core_copy(x, zs).start())
        if n >= lag:
            take_x((z + ORDER[n - lag]) % NZ)

    for zs in range(NZ):
        arrived(qr_ref.at[pl.ds(0, 3), zs], z_recv.at[zs, 2])
        pl.when(has_extra)(lambda: arrived(qr_ref.at[3, zs], z_recv.at[zs, 3]))

    def xq_copies(act):
        for dx in range(NX):
            xt = (x + dx) % NX

            def away():
                if dx:
                    copy = remote(
                        qr_ref.at[xt], qf_ref.at[x], xq_send.at[dx], xq_recv.at[x], z * NX + xt, 2 * y + c
                    )
                    if act == "start":
                        copy.start()
                    else:
                        copy.wait_send()
                elif act == "start":
                    pltpu.make_async_copy(qr_ref.at[x], qf_ref.at[x], xq_recv.at[x]).start()

            pl.when((xt != 3) | has_extra)(away)

    xq_copies("start")
    for n in range(NZ - lag, NZ):
        take_x((z + ORDER[n]) % NZ)

    @pl.when(member)
    def _():
        for xs in range(NX):
            arrived(qf_ref.at[xs], xq_recv.at[xs])
        for xs in range(NX):
            for zs in range(NZ):
                arrived(kv_ref.at[1 - c, xs, zs], c_recv.at[xs, zs])
                core_copy(xs, zs).wait_send()

    z_copies("wait")
    for n, dz in enumerate(ORDER):
        x_copies(n, (z + dz) % NZ, "wait")
    xq_copies("wait")


def spread(query_states, key_states, value_states):
    bf16 = jnp.bfloat16
    any_spec = pl.BlockSpec(memory_space=pl.ANY)
    dma = pltpu.SemaphoreType.DMA
    kv, qf, _ = pl.pallas_call(
        spread_kernel,
        out_shape=(
            jax.ShapeDtypeStruct((2, 5, NZ, ROWS, HEAD_DIM), bf16),
            jax.ShapeDtypeStruct((NX, NZ, CUBE, HEAD_DIM), bf16),
            jax.ShapeDtypeStruct((NX, NZ, CUBE, HEAD_DIM), bf16),
        ),
        in_specs=[any_spec] * 3,
        out_specs=(any_spec,) * 3,
        scratch_shapes=[
            dma((NZ, 2, 4)), dma((NZ, 4)),
            dma((NX, NZ)), dma((NX, NZ)),
            dma((NX,)), dma((NX,)),
            dma((NX, NZ)), dma((NX, NZ)),
        ],
        compiler_params=pltpu.CompilerParams(collective_id=0, has_side_effects=True),
        name="spread",
    )(query_states.reshape(3, 2, CUBE, HEADS_DEV * HEAD_DIM), key_states, value_states)
    return kv, qf


def collect_kernel(o_ref, a_ref, relay_ref, x_send, x_recv, z_send, z_recv):
    z, x, y, c = place()
    has_extra = z % 4 != 3
    member = (x != 3) | has_extra
    greet(z, x, y, c)

    def x_copies(act):
        for dx in range(NX):
            xt = (x + dx) % NX
            if dx:
                copy = remote(
                    o_ref.at[xt], relay_ref.at[x], x_send.at[dx], x_recv.at[x], z * NX + xt, 2 * y + c
                )
                if act == "start":
                    copy.start()
                else:
                    copy.wait_send()
            elif act == "start":
                pltpu.make_async_copy(o_ref.at[x], relay_ref.at[x], x_recv.at[x]).start()

    pl.when(member)(lambda: x_copies("start"))
    for xs in range(3):
        arrived(relay_ref.at[xs], x_recv.at[xs])
    pl.when(has_extra)(lambda: arrived(relay_ref.at[3], x_recv.at[3]))

    def z_copies(act):
        for n, dz in enumerate(ORDER):
            zt = (z + dz) % NZ

            def one(cond, kind, core, src, dst):
                def away():
                    copy = remote(
                        src, dst, z_send.at[n, kind], z_recv.at[z, c, kind], zt * NX + x, 2 * y + core
                    )
                    if act == "start":
                        copy.start()
                    else:
                        copy.wait_send()

                if dz:
                    pl.when(cond)(away)
                else:
                    pl.when(cond & (c != core))(away)
                    if act == "start":
                        pl.when(cond & (c == core))(
                            lambda: pltpu.make_async_copy(src, dst, z_recv.at[z, c, kind]).start()
                        )

            col = pl.ds(pl.multiple_of(z % 5 * HEAD_DIM, HEAD_DIM), HEAD_DIM)
            one(z >= 0, 0, z // 5, relay_ref.at[pl.ds(0, 3), zt], a_ref.at[:, c, :, col])
            xcol = pl.ds(pl.multiple_of((3 + z // 4) * HEAD_DIM, HEAD_DIM), HEAD_DIM)
            rank = z % 4 - z % 4 // 3
            one(has_extra, 1, 1, relay_ref.at[3, zt], a_ref.at[rank, c, :, xcol])

    z_copies("start")
    for zs in range(NZ):
        for cc in range(2):
            col = pl.ds(zs % 5 * HEAD_DIM, HEAD_DIM)
            pl.when(c == zs // 5)(lambda: arrived(a_ref.at[:, cc, :, col], z_recv.at[zs, cc, 0]))
            if zs % 4 != 3:
                xcol = pl.ds((3 + zs // 4) * HEAD_DIM, HEAD_DIM)
                pl.when(c == 1)(lambda: arrived(a_ref.at[zs % 4, cc, :, xcol], z_recv.at[zs, cc, 1]))
    pl.when(member)(lambda: x_copies("wait"))
    z_copies("wait")


def collect(outputs):
    bf16 = jnp.bfloat16
    any_spec = pl.BlockSpec(memory_space=pl.ANY)
    dma = pltpu.SemaphoreType.DMA
    attended, _ = pl.pallas_call(
        collect_kernel,
        out_shape=(
            jax.ShapeDtypeStruct((3, 2, CUBE, HEADS_DEV * HEAD_DIM), bf16),
            jax.ShapeDtypeStruct((NX, NZ, CUBE, HEAD_DIM), bf16),
        ),
        in_specs=[any_spec],
        out_specs=(any_spec,) * 2,
        scratch_shapes=[dma((NX,)), dma((NX,)), dma((NZ, 2)), dma((NZ, 2, 2))],
        compiler_params=pltpu.CompilerParams(collective_id=1, has_side_effects=True),
        name="collect",
    )(outputs)
    return attended.reshape(ROWS, HEADS_DEV * HEAD_DIM)


CONTRACT_LAST = (((1,), (1,)), ((), ()))
N_CUBES = NZ * NX * CUBE_DEV


def attend_kernel(sel_ref, kv_ref, q_ref, o_ref, pooled, scores):
    f32, bf16 = jnp.float32, jnp.bfloat16

    def pool(i, _):
        for a in range(2):
            block = kv_ref[a, pl.ds(pl.multiple_of(i * 1024, 1024), 1024), :].astype(f32)
            sums = jnp.sum(block.reshape(16, CUBE, HEAD_DIM), axis=1)
            pooled[a, pl.ds(pl.multiple_of(i * 16, 16), 16), :] = (sums * (1.0 / CUBE)).astype(bf16)
        return 0

    lax.fori_loop(0, N_CUBES // 16, pool, 0)
    group = 4
    width = group * CUBE

    def rows(a, t, g):
        tiles = [
            kv_ref[a, pl.ds(pl.multiple_of(sel_ref[t, g * group + n] * CUBE, CUBE), CUBE), :]
            for n in range(group)
        ]
        return jnp.concatenate(tiles, axis=0)

    def score(t, u):
        q = q_ref[t]
        top = None
        for g in range(TOPK // group):
            s = lax.dot_general(q, rows(0, t, g), CONTRACT_LAST, preferred_element_type=f32)
            scores[u, :, g * width:(g + 1) * width] = s
            part = jnp.maximum(s[:, :128], s[:, 128:])
            top = part if top is None else jnp.maximum(top, part)
        return q, jnp.max(top, axis=1, keepdims=True)

    def mix(t, u, q, top):
        acc = jnp.zeros((CUBE, HEAD_DIM), f32)
        total = jnp.zeros((CUBE, 128), f32)
        for g in range(TOPK // group):
            s = scores[u, :, g * width:(g + 1) * width]
            e = jnp.exp2((s - top) * EXP_SCALE)
            total = total + (e[:, :128] + e[:, 128:])
            acc = acc + jnp.dot(e.astype(bf16), rows(1, t, g), preferred_element_type=f32)
        fine = acc / jnp.sum(total, axis=1, keepdims=True)
        s = lax.dot_general(q, pooled[0], CONTRACT_LAST, preferred_element_type=f32)
        e = jnp.exp2((s - jnp.max(s, axis=1, keepdims=True)) * EXP_SCALE)
        coarse = jnp.dot(e.astype(bf16), pooled[1], preferred_element_type=f32)
        coarse = coarse / jnp.sum(e, axis=1, keepdims=True)
        o_ref[t] = (fine + coarse).astype(bf16)

    unroll = 2

    def step(i, _):
        held = [score(i * unroll + u, u) for u in range(unroll)]
        for u in range(unroll):
            mix(i * unroll + u, u, *held[u])
        return 0

    lax.fori_loop(0, NZ * NX // unroll, step, 0)


def attend(positions, kv, queries):
    bf16 = jnp.bfloat16
    whole = lambda *shape: pl.BlockSpec(shape, lambda i: (0,) * len(shape))
    return pl.pallas_call(
        attend_kernel,
        grid=(1,),
        out_shape=jax.ShapeDtypeStruct((NZ * NX, CUBE, HEAD_DIM), bf16),
        in_specs=[
            pl.BlockSpec(memory_space=pltpu.SMEM),
            whole(2, NZ * NX * ROWS, HEAD_DIM),
            whole(NZ * NX, CUBE, HEAD_DIM),
        ],
        out_specs=whole(NZ * NX, CUBE, HEAD_DIM),
        scratch_shapes=[
            pltpu.VMEM((2, N_CUBES, HEAD_DIM), bf16),
            pltpu.VMEM((2, CUBE, TOPK * CUBE), jnp.float32),
        ],
        compiler_params=pltpu.CompilerParams(vmem_limit_bytes=48 * 2**20),
        name="attend",
    )(positions, kv, queries)


def my_positions(selection):
    z, x, _, c = place()
    everyone = lax.all_gather(selection, "seq", axis=0, tiled=True)
    rank = x + x // 3 * (z % 4 - x)
    cube = jnp.minimum(2 * rank + c, CUBE_DEV - 1)
    mine = lax.dynamic_index_in_dim(everyone.reshape(NZ, NX, CUBE_DEV, TOPK), cube, axis=2, keepdims=False)
    mine = mine.transpose(1, 0, 2).reshape(NZ * NX, TOPK)
    owner = mine // CUBE_DEV
    return (owner % NX * NZ + owner // NX) * CUBE_DEV + mine % CUBE_DEV


def body(query_states, key_states, value_states, gate_states, selection, out_weight):
    positions = my_positions(selection)
    kv, queries = spread(query_states, key_states, value_states)
    kv = kv.reshape(2, 5 * NZ * ROWS, HEAD_DIM)
    outputs = attend(positions, kv, queries.reshape(NZ * NX, CUBE, HEAD_DIM))
    mixed = collect(outputs.reshape(NX, NZ, CUBE, HEAD_DIM))
    gates = jax.nn.sigmoid(gate_states.astype(jnp.float32))
    attended = (gates * mixed.astype(jnp.float32)).astype(jnp.bfloat16)
    return lax.psum_scatter(
        jnp.dot(attended, out_weight, preferred_element_type=jnp.float32).astype(jnp.bfloat16),
        "head",
        scatter_dimension=0,
        tiled=True,
    )


def solution(mesh):
    placed = (
        P("seq", "head"),
        P("seq", "head"),
        P("seq", "head"),
        P("seq", "head"),
        P("seq", None),
        P("head", None),
    )
    return jax.shard_map(
        body, mesh=mesh, in_specs=placed, out_specs=P(("seq", "head"), None), check_vma=False
    )
```

```python
import functools
import math

import jax
import jax.numpy as jnp
from jax import lax
from jax.experimental import pallas as pl
from jax.experimental.pallas import tpu as pltpu
from jax.sharding import PartitionSpec as P

MESH = pl.DeviceIdType.MESH
HEAD_DIM = 128
CUBE = 64
CUBE_DEV = 6
TOPK = 32
NZ, NX = 8, 4
ROWS = CUBE * CUBE_DEV
HEADS_DEV = 5
ORDER = (0, 1, 7, 2, 6, 3, 5, 4)
XORDER = (1, 3, 2)
EXP_SCALE = HEAD_DIM ** (-0.5) * math.log2(math.e)


def place():
    seq, head = lax.axis_index("seq"), lax.axis_index("head")
    return seq // NX, seq % NX, head // 2, head % 2


def remote(src, dst, send_sem, recv_sem, seq, head):
    return pltpu.make_async_remote_copy(
        src_ref=src,
        dst_ref=dst,
        send_sem=send_sem,
        recv_sem=recv_sem,
        device_id={"seq": seq, "head": head},
        device_id_type=MESH,
    )


def arrived(ref, sem):
    pltpu.make_async_copy(ref, ref, sem).wait()


def greet(z, x, y, c, with_y=False):
    barrier = pltpu.get_barrier_semaphore()
    for dz in range(NZ):
        for dc in range(2):
            if dz or dc:
                pl.semaphore_signal(
                    barrier,
                    inc=1,
                    device_id={"seq": (z + dz) % NZ * NX + x, "head": 2 * y + (c + dc) % 2},
                    device_id_type=MESH,
                )
    for dx in range(1, NX):
        pl.semaphore_signal(
            barrier,
            inc=1,
            device_id={"seq": z * NX + (x + dx) % NX, "head": 2 * y + c},
            device_id_type=MESH,
        )
    if with_y:
        for dy in (1, 3):
            pl.semaphore_signal(
                barrier,
                inc=1,
                device_id={"seq": z * NX + x, "head": 2 * ((y + dy) % 4) + c},
                device_id_type=MESH,
            )
    pl.semaphore_wait(barrier, 2 * NZ - 1 + NX - 1 + (2 if with_y else 0))


def spread_kernel(
    sel_ref, q_ref, k_ref, v_ref, kv_ref, qf_ref, all_sel_ref, qr_ref,
    z_send, z_recv, x_send, x_recv, xq_send, xq_recv, c_send, c_recv,
    sz_send, sz_recv, sx_send, sx_recv,
):
    z, x, y, c = place()
    here = z * NX + x
    sibling = 2 * y + 1 - c
    main_slot = x + x // 3
    extra_slot = 4 - x // 3
    has_extra = z % 4 != 3
    member = (x != 3) | has_extra
    greet(z, x, y, c)

    def sel_z(n, dz):
        return remote(
            sel_ref, all_sel_ref.at[x, z], sz_send.at[n], sz_recv.at[z], (z + dz) % NZ * NX + x, 2 * y + c
        )

    def sel_x(dx):
        return remote(
            all_sel_ref.at[x], all_sel_ref.at[x], sx_send.at[dx], sx_recv.at[x], z * NX + (x + dx) % NX, 2 * y + c
        )

    pltpu.make_async_copy(sel_ref, all_sel_ref.at[x, z], sz_recv.at[z]).start()
    for n, dz in enumerate(ORDER):
        if dz:
            sel_z(n, dz).start()

    def z_copies(act):
        for n, dz in enumerate(ORDER):
            zt = (z + dz) % NZ
            for cc in range(2):
                source = k_ref if cc == 0 else v_ref

                def one(cond, kind, src, dst):
                    def away():
                        copy = remote(
                            src, dst, z_send.at[n, cc, kind], z_recv.at[z, kind], zt * NX + x, 2 * y + cc
                        )
                        if act == "start":
                            copy.start()
                        else:
                            copy.wait_send()

                    if dz:
                        pl.when(cond)(away)
                    else:
                        pl.when(cond & (c != cc))(away)
                        if act == "start":
                            pl.when(cond & (c == cc))(
                                lambda: pltpu.make_async_copy(src, dst, z_recv.at[z, kind]).start()
                            )

                is_main = c == zt // 5
                col = pl.ds(pl.multiple_of(zt % 5 * HEAD_DIM, HEAD_DIM), HEAD_DIM)
                one(is_main, 0, source.at[:, col], kv_ref.at[cc, main_slot, z])
                is_extra = (c == 1) & (zt % 4 != 3)
                xcol = pl.ds(pl.multiple_of((3 + zt // 4) * HEAD_DIM, HEAD_DIM), HEAD_DIM)
                one(is_extra, 1, source.at[:, xcol], kv_ref.at[cc, extra_slot, z])
                one(is_main, 2, q_ref.at[:, cc, :, col], qr_ref.at[pl.ds(0, 3), z])
                rank = zt % 4 - zt % 4 // 3
                one(is_extra, 3, q_ref.at[rank, cc, :, xcol], qr_ref.at[3, z])

    z_copies("start")
    for zs in range(NZ):
        arrived(all_sel_ref.at[x, zs], sz_recv.at[zs])
    for dx in range(1, NX):
        sel_x(dx).start()

    def x_copies(n, zs, act):
        for dx in XORDER:
            xt = (x + dx) % NX
            slot = main_slot + xt // 3 * (4 - main_slot)

            def away():
                copy = remote(
                    kv_ref.at[c, slot, zs], kv_ref.at[c, x, zs],
                    x_send.at[dx, n], x_recv.at[x, zs], z * NX + xt, 2 * y + c,
                )
                if act == "start":
                    copy.start()
                else:
                    copy.wait_send()

            pl.when((xt != 3) | has_extra)(away)

    def core_copy(xs, zs):
        return remote(
            kv_ref.at[c, xs, zs], kv_ref.at[c, xs, zs],
            c_send.at[xs, zs], c_recv.at[xs, zs], here, sibling,
        )

    def take_x(zs):
        for dx in XORDER:
            xs = (x + dx) % NX

            @pl.when(member)
            def _():
                arrived(kv_ref.at[c, xs, zs], x_recv.at[xs, zs])
                core_copy(xs, zs).start()

    lag = 2
    for n, dz in enumerate(ORDER):
        zs = (z + dz) % NZ
        arrived(kv_ref.at[c, main_slot, zs], z_recv.at[zs, 0])
        pl.when(has_extra)(lambda: arrived(kv_ref.at[c, extra_slot, zs], z_recv.at[zs, 1]))
        x_copies(n, zs, "start")
        pl.when(member)(lambda: core_copy(x, zs).start())
        if n >= lag:
            take_x((z + ORDER[n - lag]) % NZ)

    for zs in range(NZ):
        arrived(qr_ref.at[pl.ds(0, 3), zs], z_recv.at[zs, 2])
        pl.when(has_extra)(lambda: arrived(qr_ref.at[3, zs], z_recv.at[zs, 3]))

    def xq_copies(act):
        for dx in range(NX):
            xt = (x + dx) % NX

            def away():
                if dx:
                    copy = remote(
                        qr_ref.at[xt], qf_ref.at[x], xq_send.at[dx], xq_recv.at[x], z * NX + xt, 2 * y + c
                    )
                    if act == "start":
                        copy.start()
                    else:
                        copy.wait_send()
                elif act == "start":
                    pltpu.make_async_copy(qr_ref.at[x], qf_ref.at[x], xq_recv.at[x]).start()

            pl.when((xt != 3) | has_extra)(away)

    xq_copies("start")
    for n in range(NZ - lag, NZ):
        take_x((z + ORDER[n]) % NZ)

    @pl.when(member)
    def _():
        for xs in range(NX):
            arrived(qf_ref.at[xs], xq_recv.at[xs])
        for xs in range(NX):
            for zs in range(NZ):
                arrived(kv_ref.at[1 - c, xs, zs], c_recv.at[xs, zs])
                core_copy(xs, zs).wait_send()

    for dx in range(1, NX):
        arrived(all_sel_ref.at[(x + dx) % NX], sx_recv.at[(x + dx) % NX])
        sel_x(dx).wait_send()
    for n, dz in enumerate(ORDER):
        if dz:
            sel_z(n, dz).wait_send()
    z_copies("wait")
    for n, dz in enumerate(ORDER):
        x_copies(n, (z + dz) % NZ, "wait")
    xq_copies("wait")


def spread(selection, query_states, key_states, value_states):
    bf16 = jnp.bfloat16
    any_spec = pl.BlockSpec(memory_space=pl.ANY)
    dma = pltpu.SemaphoreType.DMA
    kv, qf, all_sel, _ = pl.pallas_call(
        spread_kernel,
        out_shape=(
            jax.ShapeDtypeStruct((2, 5, NZ, ROWS, HEAD_DIM), bf16),
            jax.ShapeDtypeStruct((NX, NZ, CUBE, HEAD_DIM), bf16),
            jax.ShapeDtypeStruct((NX, NZ, CUBE_DEV, TOPK), jnp.int32),
            jax.ShapeDtypeStruct((NX, NZ, CUBE, HEAD_DIM), bf16),
        ),
        in_specs=[any_spec] * 4,
        out_specs=(any_spec,) * 4,
        scratch_shapes=[
            dma((NZ, 2, 4)), dma((NZ, 4)),
            dma((NX, NZ)), dma((NX, NZ)),
            dma((NX,)), dma((NX,)),
            dma((NX, NZ)), dma((NX, NZ)),
            dma((NZ,)), dma((NZ,)), dma((NX,)), dma((NX,)),
        ],
        compiler_params=pltpu.CompilerParams(collective_id=0, has_side_effects=True),
        name="spread",
    )(selection, query_states.reshape(3, 2, CUBE, HEADS_DEV * HEAD_DIM), key_states, value_states)
    return kv, qf, all_sel


NY = 4
FEATS = HEADS_DEV * HEAD_DIM
BAND = ROWS // NY
BAND_CORE = BAND // 2
COLS = 2560
TILE = 640
TILES = COLS // TILE


def finish_kernel(
    o_ref, gate_ref, w_ref, out_ref,
    relay_ref, a_ref, att, weight, part, passed, landed, done,
    x_send, x_recv, z_send, z_recv, w_sem, t_sem,
    part_send, passed_recv, landed_recv, done_send, done_recv,
):
    f32, bf16 = jnp.float32, jnp.bfloat16
    z, x, y, c = place()
    here = z * NX + x
    has_extra = z % 4 != 3
    member = (x != 3) | has_extra
    greet(z, x, y, c, True)

    def x_copies(act):
        for dx in range(NX):
            xt = (x + dx) % NX
            if dx:
                copy = remote(
                    o_ref.at[xt], relay_ref.at[x], x_send.at[dx], x_recv.at[x], z * NX + xt, 2 * y + c
                )
                if act == "start":
                    copy.start()
                else:
                    copy.wait_send()
            elif act == "start":
                pltpu.make_async_copy(o_ref.at[x], relay_ref.at[x], x_recv.at[x]).start()

    pl.when(member)(lambda: x_copies("start"))

    def half(core):
        return pl.ds(pl.multiple_of(core * COLS, COLS), COLS)

    def block(core):
        return pl.ds(pl.multiple_of(core * FEATS, FEATS), FEATS)

    w_own = pltpu.make_async_copy(w_ref.at[:, half(c)], weight.at[block(c)], w_sem.at[0])
    w_away = remote(
        w_ref.at[:, half(1 - c)], weight.at[block(c)], w_sem.at[1], w_sem.at[2], here, 2 * y + 1 - c
    )
    w_own.start()
    w_away.start()

    for xs in range(3):
        arrived(relay_ref.at[xs], x_recv.at[xs])
    pl.when(has_extra)(lambda: arrived(relay_ref.at[3], x_recv.at[3]))

    def z_copies(act):
        for n, dz in enumerate(ORDER):
            zt = (z + dz) % NZ

            def one(cond, kind, core, src, dst):
                def away():
                    copy = remote(
                        src, dst, z_send.at[n, kind], z_recv.at[z, c, kind], zt * NX + x, 2 * y + core
                    )
                    if act == "start":
                        copy.start()
                    else:
                        copy.wait_send()

                if dz:
                    pl.when(cond)(away)
                else:
                    pl.when(cond & (c != core))(away)
                    if act == "start":
                        pl.when(cond & (c == core))(
                            lambda: pltpu.make_async_copy(src, dst, z_recv.at[z, c, kind]).start()
                        )

            col = pl.ds(pl.multiple_of(z % 5 * HEAD_DIM, HEAD_DIM), HEAD_DIM)
            one(z >= 0, 0, z // 5, relay_ref.at[pl.ds(0, 3), zt], a_ref.at[:, c, :, col])
            xcol = pl.ds(pl.multiple_of((3 + z // 4) * HEAD_DIM, HEAD_DIM), HEAD_DIM)
            rank = z % 4 - z % 4 // 3
            one(has_extra, 1, 1, relay_ref.at[3, zt], a_ref.at[rank, c, :, xcol])

    z_copies("start")
    for zs in range(NZ):
        for cc in range(2):
            col = pl.ds(zs % 5 * HEAD_DIM, HEAD_DIM)
            pl.when(c == zs // 5)(lambda: arrived(a_ref.at[:, cc, :, col], z_recv.at[zs, cc, 0]))
            if zs % 4 != 3:
                xcol = pl.ds((3 + zs // 4) * HEAD_DIM, HEAD_DIM)
                pl.when(c == 1)(lambda: arrived(a_ref.at[zs % 4, cc, :, xcol], z_recv.at[zs, cc, 1]))

    mixed = a_ref[...].reshape(ROWS, FEATS).astype(f32)
    att[c] = (jax.nn.sigmoid(gate_ref[...].astype(f32)) * mixed).astype(bf16)
    att_away = remote(att.at[c], att.at[c], t_sem.at[0], t_sem.at[1], here, 2 * y + 1 - c)
    att_away.start()
    w_own.wait()
    arrived(weight.at[block(1 - c)], w_sem.at[2])
    arrived(att.at[1 - c], t_sem.at[1])

    def product(band, t):
        rows = pl.ds(pl.multiple_of(band * BAND, BAND), BAND)
        cols = slice(t * TILE, (t + 1) * TILE)
        total = jnp.dot(att[0, rows, :], weight[:FEATS, cols], preferred_element_type=f32)
        return total + jnp.dot(att[1, rows, :], weight[FEATS:, cols], preferred_element_type=f32)

    right, left = (y + 1) % NY, (y + 3) % NY

    def across(t):
        return remote(
            part.at[1, t], passed.at[t], part_send.at[1, t], passed_recv.at[t],
            here, 2 * (right if t < 2 else left) + c,
        )

    def onward(side, t):
        return remote(
            part.at[2 * side, t], landed.at[side, t], part_send.at[2 * side, t], landed_recv.at[side, t],
            here, 2 * (left if side else right) + c,
        )

    for t in (0, 2, 1, 3):
        part[1, t] = product((y + 2) % NY, t).astype(bf16)
        across(t).start()
    for side, t in ((0, 2), (1, 0), (0, 3), (1, 1)):
        part[2 * side, t] = product(left if side else right, t).astype(bf16)
        onward(side, t).start()
    for side, t in ((0, 0), (1, 2), (0, 1), (1, 3)):
        total = product(left if side else right, t)
        arrived(passed.at[t], passed_recv.at[t])
        part[2 * side, t] = (total + passed[t].astype(f32)).astype(bf16)
        onward(side, t).start()

    def rows_of(core):
        return pl.ds(pl.multiple_of(core * BAND_CORE, BAND_CORE), BAND_CORE)

    def columns(core, t):
        return pl.ds(pl.multiple_of(core * COLS + t * TILE, TILE), TILE)

    def give(t):
        return remote(
            done.at[t, rows_of(1 - c)], out_ref.at[:, columns(c, t)],
            done_send.at[0, t], done_recv.at[t], here, 2 * y + 1 - c,
        )

    def keep(t):
        return pltpu.make_async_copy(done.at[t, rows_of(c)], out_ref.at[:, columns(c, t)], done_send.at[1, t])

    for t in (2, 0, 3, 1):
        total = product(y, t)
        for side in range(2):
            arrived(landed.at[side, t], landed_recv.at[side, t])
            total = total + landed[side, t].astype(f32)
        done[t] = total.astype(bf16)
        give(t).start()
        keep(t).start()

    for t in range(TILES):
        give(t).wait_send()
        keep(t).wait()
        arrived(out_ref.at[:, columns(1 - c, t)], done_recv.at[t])
        across(t).wait_send()
        for side in range(2):
            onward(side, t).wait_send()
    w_away.wait_send()
    att_away.wait_send()
    pl.when(member)(lambda: x_copies("wait"))
    z_copies("wait")


def finish(outputs, gate_states, out_weight):
    bf16 = jnp.bfloat16
    any_spec = pl.BlockSpec(memory_space=pl.ANY)
    dma, vmem = pltpu.SemaphoreType.DMA, pltpu.VMEM
    return pl.pallas_call(
        finish_kernel,
        out_shape=jax.ShapeDtypeStruct((BAND_CORE, 2 * COLS), bf16),
        in_specs=[any_spec, pl.BlockSpec(memory_space=pltpu.VMEM), any_spec],
        out_specs=any_spec,
        scratch_shapes=[
            vmem((NX, NZ, CUBE, HEAD_DIM), bf16),
            vmem((3, 2, CUBE, FEATS), bf16),
            vmem((2, ROWS, FEATS), bf16),
            vmem((2 * FEATS, COLS), bf16),
            vmem((3, TILES, BAND, TILE), bf16),
            vmem((TILES, BAND, TILE), bf16),
            vmem((2, TILES, BAND, TILE), bf16),
            vmem((TILES, BAND, TILE), bf16),
            dma((NX,)), dma((NX,)), dma((NZ, 2)), dma((NZ, 2, 2)), dma((3,)), dma((2,)),
            dma((3, TILES)), dma((TILES,)), dma((2, TILES)), dma((2, TILES)), dma((TILES,)),
        ],
        compiler_params=pltpu.CompilerParams(
            collective_id=1, has_side_effects=True, vmem_limit_bytes=40 * 2**20
        ),
        name="finish",
    )(outputs, gate_states, out_weight)


CONTRACT_LAST = (((1,), (1,)), ((), ()))
N_CUBES = NZ * NX * CUBE_DEV


def attend_kernel(sel_ref, kv_ref, q_ref, o_ref, pooled, scores):
    f32, bf16 = jnp.float32, jnp.bfloat16

    def pool(i, _):
        for a in range(2):
            block = kv_ref[a, pl.ds(pl.multiple_of(i * 1024, 1024), 1024), :].astype(f32)
            sums = jnp.sum(block.reshape(16, CUBE, HEAD_DIM), axis=1)
            pooled[a, pl.ds(pl.multiple_of(i * 16, 16), 16), :] = (sums * (1.0 / CUBE)).astype(bf16)
        return 0

    lax.fori_loop(0, N_CUBES // 16, pool, 0)
    group = 4
    width = group * CUBE

    def rows(a, t, g):
        tiles = [
            kv_ref[a, pl.ds(pl.multiple_of(sel_ref[t, g * group + n] * CUBE, CUBE), CUBE), :]
            for n in range(group)
        ]
        return jnp.concatenate(tiles, axis=0)

    def score(t, u):
        q = q_ref[t]
        top = None
        for g in range(TOPK // group):
            s = lax.dot_general(q, rows(0, t, g), CONTRACT_LAST, preferred_element_type=f32)
            scores[u, :, g * width:(g + 1) * width] = s
            part = jnp.maximum(s[:, :128], s[:, 128:])
            top = part if top is None else jnp.maximum(top, part)
        return q, jnp.max(top, axis=1, keepdims=True)

    def mix(t, u, q, top):
        acc = jnp.zeros((CUBE, HEAD_DIM), f32)
        total = jnp.zeros((CUBE, 128), f32)
        for g in range(TOPK // group):
            s = scores[u, :, g * width:(g + 1) * width]
            e = jnp.exp2((s - top) * EXP_SCALE)
            total = total + (e[:, :128] + e[:, 128:])
            acc = acc + jnp.dot(e.astype(bf16), rows(1, t, g), preferred_element_type=f32)
        fine = acc / jnp.sum(total, axis=1, keepdims=True)
        s = lax.dot_general(q, pooled[0], CONTRACT_LAST, preferred_element_type=f32)
        e = jnp.exp2((s - jnp.max(s, axis=1, keepdims=True)) * EXP_SCALE)
        coarse = jnp.dot(e.astype(bf16), pooled[1], preferred_element_type=f32)
        coarse = coarse / jnp.sum(e, axis=1, keepdims=True)
        o_ref[t] = (fine + coarse).astype(bf16)

    unroll = 2

    def step(i, _):
        held = [score(i * unroll + u, u) for u in range(unroll)]
        for u in range(unroll):
            mix(i * unroll + u, u, *held[u])
        return 0

    lax.fori_loop(0, NZ * NX // unroll, step, 0)


def attend(positions, kv, queries):
    bf16 = jnp.bfloat16
    whole = lambda *shape: pl.BlockSpec(shape, lambda i: (0,) * len(shape))
    return pl.pallas_call(
        attend_kernel,
        grid=(1,),
        out_shape=jax.ShapeDtypeStruct((NZ * NX, CUBE, HEAD_DIM), bf16),
        in_specs=[
            pl.BlockSpec(memory_space=pltpu.SMEM),
            whole(2, NZ * NX * ROWS, HEAD_DIM),
            whole(NZ * NX, CUBE, HEAD_DIM),
        ],
        out_specs=whole(NZ * NX, CUBE, HEAD_DIM),
        scratch_shapes=[
            pltpu.VMEM((2, N_CUBES, HEAD_DIM), bf16),
            pltpu.VMEM((2, CUBE, TOPK * CUBE), jnp.float32),
        ],
        compiler_params=pltpu.CompilerParams(vmem_limit_bytes=48 * 2**20),
        name="attend",
    )(positions, kv, queries)


def my_positions(all_sel):
    z, x, _, c = place()
    rank = x + x // 3 * (z % 4 - x)
    cube = jnp.minimum(2 * rank + c, CUBE_DEV - 1)
    mine = lax.dynamic_index_in_dim(all_sel, cube, axis=2, keepdims=False).reshape(NZ * NX, TOPK)
    owner = mine // CUBE_DEV
    return (owner % NX * NZ + owner // NX) * CUBE_DEV + mine % CUBE_DEV


def body(query_states, key_states, value_states, gate_states, selection, out_weight):
    kv, queries, all_sel = spread(selection, query_states, key_states, value_states)
    kv = kv.reshape(2, 5 * NZ * ROWS, HEAD_DIM)
    outputs = attend(my_positions(all_sel), kv, queries.reshape(NZ * NX, CUBE, HEAD_DIM))
    return finish(outputs.reshape(NX, NZ, CUBE, HEAD_DIM), gate_states, out_weight)


def solution(mesh):
    placed = (
        P("seq", "head"),
        P("seq", "head"),
        P("seq", "head"),
        P("seq", "head"),
        P("seq", None),
        P("head", None),
    )
    return jax.shard_map(
        body, mesh=mesh, in_specs=placed, out_specs=P(("seq", "head"), None), check_vma=False
    )
```

```python
import functools
import math

import jax
import jax.numpy as jnp
from jax import lax
from jax.experimental import pallas as pl
from jax.experimental.pallas import tpu as pltpu
from jax.sharding import PartitionSpec as P

MESH = pl.DeviceIdType.MESH
HEAD_DIM = 128
CUBE = 64
CUBE_DEV = 6
TOPK = 32
NZ, NX = 8, 4
ROWS = CUBE * CUBE_DEV
HEADS_DEV = 5
NY = 4
ORDER = (0, 1, 7, 2, 6, 3, 5, 4)
XORDER = (1, 3, 2)
FEATS = HEADS_DEV * HEAD_DIM
BAND = ROWS // NY
BAND_CORE = BAND // 2
COLS = 2560
TILE = 640
TILES = COLS // TILE
N_CUBES = NZ * NX * CUBE_DEV
GROUP = 4
WIDTH = GROUP * CUBE
LAG = 2
CONTRACT_LAST = (((1,), (1,)), ((), ()))
EXP_SCALE = HEAD_DIM ** (-0.5) * math.log2(math.e)


def place():
    seq, head = lax.axis_index("seq"), lax.axis_index("head")
    return seq // NX, seq % NX, head // 2, head % 2


def remote(src, dst, send_sem, recv_sem, seq, head):
    return pltpu.make_async_remote_copy(
        src_ref=src,
        dst_ref=dst,
        send_sem=send_sem,
        recv_sem=recv_sem,
        device_id={"seq": seq, "head": head},
        device_id_type=MESH,
    )


def arrived(ref, sem):
    pltpu.make_async_copy(ref, ref, sem).wait()


def greet(z, x, y, c):
    barrier = pltpu.get_barrier_semaphore()
    for dz in range(NZ):
        for dc in range(2):
            if dz or dc:
                pl.semaphore_signal(
                    barrier,
                    inc=1,
                    device_id={"seq": (z + dz) % NZ * NX + x, "head": 2 * y + (c + dc) % 2},
                    device_id_type=MESH,
                )
    for dx in range(1, NX):
        pl.semaphore_signal(
            barrier,
            inc=1,
            device_id={"seq": z * NX + (x + dx) % NX, "head": 2 * y + c},
            device_id_type=MESH,
        )
    for dy in (1, 3):
        pl.semaphore_signal(
            barrier,
            inc=1,
            device_id={"seq": z * NX + x, "head": 2 * ((y + dy) % NY) + c},
            device_id_type=MESH,
        )
    pl.semaphore_wait(barrier, 2 * NZ - 1 + NX - 1 + 2)


def kernel(
    sel_ref, q_ref, k_ref, v_ref, gate_ref, w_ref, out_ref,
    kv_ref, qr_ref, qf_ref, all_sel_ref, sel, pooled, scores, o_ref,
    relay_ref, a_ref, att, weight, part, passed, landed, done,
    z_send, z_recv, x_send, x_recv, xq_send, xq_recv, c_send, c_recv,
    sz_send, sz_recv, sx_send, sx_recv, pick_sem,
    o_send, o_recv, r_send, r_recv, w_sem, t_sem,
    part_send, passed_recv, landed_recv, done_send, done_recv,
):
    f32, bf16 = jnp.float32, jnp.bfloat16
    z, x, y, c = place()
    here = z * NX + x
    sibling = 2 * y + 1 - c
    main_slot = x + x // 3
    extra_slot = 4 - x // 3
    has_extra = z % 4 != 3
    member = (x != 3) | has_extra
    greet(z, x, y, c)

    def tile_at(which, slot, zs):
        return kv_ref.at[which, pl.ds((slot * NZ + zs) * CUBE_DEV, CUBE_DEV)]

    def half(core):
        return pl.ds(pl.multiple_of(core * COLS, COLS), COLS)

    def block(core):
        return pl.ds(pl.multiple_of(core * FEATS, FEATS), FEATS)

    w_own = pltpu.make_async_copy(w_ref.at[:, half(c)], weight.at[block(c)], w_sem.at[0])
    w_away = remote(w_ref.at[:, half(1 - c)], weight.at[block(c)], w_sem.at[1], w_sem.at[2], here, sibling)

    def sel_z(n, dz):
        return remote(
            sel_ref, all_sel_ref.at[x, z], sz_send.at[n], sz_recv.at[z], (z + dz) % NZ * NX + x, 2 * y + c
        )

    def sel_x(dx):
        return remote(
            all_sel_ref.at[x], all_sel_ref.at[x], sx_send.at[dx], sx_recv.at[x], z * NX + (x + dx) % NX, 2 * y + c
        )

    pltpu.make_async_copy(sel_ref, all_sel_ref.at[x, z], sz_recv.at[z]).start()
    for n, dz in enumerate(ORDER):
        if dz:
            sel_z(n, dz).start()

    def z_copies(act):
        for n, dz in enumerate(ORDER):
            zt = (z + dz) % NZ
            for cc in range(2):
                source = k_ref if cc == 0 else v_ref

                def one(cond, kind, src, dst):
                    def away():
                        copy = remote(
                            src, dst, z_send.at[n, cc, kind], z_recv.at[z, kind], zt * NX + x, 2 * y + cc
                        )
                        if act == "start":
                            copy.start()
                        else:
                            copy.wait_send()

                    if dz:
                        pl.when(cond)(away)
                    else:
                        pl.when(cond & (c != cc))(away)
                        if act == "start":
                            pl.when(cond & (c == cc))(
                                lambda: pltpu.make_async_copy(src, dst, z_recv.at[z, kind]).start()
                            )

                is_main = c == zt // 5
                col = pl.ds(pl.multiple_of(zt % 5 * HEAD_DIM, HEAD_DIM), HEAD_DIM)
                one(is_main, 0, source.at[:, :, col], tile_at(cc, main_slot, z))
                is_extra = (c == 1) & (zt % 4 != 3)
                xcol = pl.ds(pl.multiple_of((3 + zt // 4) * HEAD_DIM, HEAD_DIM), HEAD_DIM)
                one(is_extra, 1, source.at[:, :, xcol], tile_at(cc, extra_slot, z))
                one(is_main, 2, q_ref.at[:, cc, :, col], qr_ref.at[pl.ds(0, 3), z])
                rank = zt % 4 - zt % 4 // 3
                one(is_extra, 3, q_ref.at[rank, cc, :, xcol], qr_ref.at[3, z])

    z_copies("start")
    w_own.start()
    w_away.start()
    for zs in range(NZ):
        arrived(all_sel_ref.at[x, zs], sz_recv.at[zs])
    for dx in range(1, NX):
        sel_x(dx).start()

    def x_copies(n, zs, act):
        for dx in XORDER:
            xt = (x + dx) % NX
            slot = main_slot + xt // 3 * (4 - main_slot)

            def away():
                copy = remote(
                    tile_at(c, slot, zs), tile_at(c, x, zs),
                    x_send.at[dx, n], x_recv.at[x, zs], z * NX + xt, 2 * y + c,
                )
                if act == "start":
                    copy.start()
                else:
                    copy.wait_send()

            pl.when((xt != 3) | has_extra)(away)

    def core_copy(xs, zs):
        return remote(
            tile_at(c, xs, zs), tile_at(c, xs, zs),
            c_send.at[xs, zs], c_recv.at[xs, zs], here, sibling,
        )

    def take_x(zs):
        for dx in XORDER:
            xs = (x + dx) % NX

            @pl.when(member)
            def _():
                arrived(tile_at(c, xs, zs), x_recv.at[xs, zs])
                core_copy(xs, zs).start()

    for n, dz in enumerate(ORDER):
        zs = (z + dz) % NZ
        arrived(tile_at(c, main_slot, zs), z_recv.at[zs, 0])
        pl.when(has_extra)(lambda: arrived(tile_at(c, extra_slot, zs), z_recv.at[zs, 1]))
        x_copies(n, zs, "start")
        pl.when(member)(lambda: core_copy(x, zs).start())
        if n >= LAG:
            take_x((z + ORDER[n - LAG]) % NZ)

    for zs in range(NZ):
        arrived(qr_ref.at[pl.ds(0, 3), zs], z_recv.at[zs, 2])
        pl.when(has_extra)(lambda: arrived(qr_ref.at[3, zs], z_recv.at[zs, 3]))

    def xq_copies(act):
        for dx in range(NX):
            xt = (x + dx) % NX

            def away():
                if dx:
                    copy = remote(
                        qr_ref.at[xt], qf_ref.at[x], xq_send.at[dx], xq_recv.at[x], z * NX + xt, 2 * y + c
                    )
                    if act == "start":
                        copy.start()
                    else:
                        copy.wait_send()
                elif act == "start":
                    pltpu.make_async_copy(qr_ref.at[x], qf_ref.at[x], xq_recv.at[x]).start()

            pl.when((xt != 3) | has_extra)(away)

    xq_copies("start")
    for n in range(NZ - LAG, NZ):
        take_x((z + ORDER[n]) % NZ)

    for dx in range(1, NX):
        arrived(all_sel_ref.at[(x + dx) % NX], sx_recv.at[(x + dx) % NX])
    picks = pltpu.make_async_copy(all_sel_ref, sel, pick_sem)
    picks.start()

    @pl.when(member)
    def _():
        for xs in range(NX):
            arrived(qf_ref.at[xs], xq_recv.at[xs])
        for xs in range(NX):
            for zs in range(NZ):
                arrived(tile_at(1 - c, xs, zs), c_recv.at[xs, zs])

    picks.wait()

    rank = x + x // 3 * (z % 4 - x)
    cube = rank * 2 + c - rank // 3 * 2

    def pool(i, _):
        for which in range(2):
            block_of = kv_ref[which, pl.ds(i * 16, 16)].astype(f32)
            sums = jnp.sum(block_of, axis=1)
            pooled[which, pl.ds(pl.multiple_of(i * 16, 16), 16), :] = (sums * (1.0 / CUBE)).astype(bf16)
        return 0

    lax.fori_loop(0, N_CUBES // 16, pool, 0)

    def target(n):
        return (z + 4 + (1 - n % 2 * 2) * ((n + 1) // 2)) % NZ

    def rows(which, xs, zs, g):
        tiles = [
            kv_ref[which, sel[xs, zs, cube, g * GROUP + n]]
            for n in range(GROUP)
        ]
        return jnp.concatenate(tiles, axis=0)

    def pair_rows(which, pair, zs, g):
        return jnp.concatenate([rows(which, 2 * pair, zs, g), rows(which, 2 * pair + 1, zs, g)], axis=1)

    def blend(pair, zs, top, pair_ahead, zs_ahead):
        acc = [jnp.zeros((CUBE, HEAD_DIM), f32) for _ in range(2)]
        total = jnp.zeros((2 * CUBE, 128), f32)
        peak = None
        if top is not None:
            q = jnp.concatenate([qf_ref[2 * pair, zs], qf_ref[2 * pair + 1, zs]], axis=0)
            s = lax.dot_general(q, pooled[0], CONTRACT_LAST, preferred_element_type=f32)
            e = jnp.exp2((s - jnp.max(s, axis=1, keepdims=True)) * EXP_SCALE)
            coarse = jnp.dot(e.astype(bf16), pooled[1], preferred_element_type=f32)
            coarse = coarse / jnp.sum(e, axis=1, keepdims=True)
        zero = jnp.zeros((CUBE, HEAD_DIM), bf16)
        ahead = jnp.concatenate([
            jnp.concatenate([qf_ref[2 * pair_ahead, zs_ahead], zero], axis=1),
            jnp.concatenate([zero, qf_ref[2 * pair_ahead + 1, zs_ahead]], axis=1),
        ], axis=0)
        for g in range(TOPK // GROUP):
            cols = slice(g * WIDTH, (g + 1) * WIDTH)
            s = lax.dot_general(ahead, pair_rows(0, pair_ahead, zs_ahead, g), CONTRACT_LAST, preferred_element_type=f32)
            scores[pair_ahead, :, cols] = s
            part_peak = jnp.maximum(s[:, :128], s[:, 128:])
            peak = part_peak if peak is None else jnp.maximum(peak, part_peak)
            if top is not None:
                e = jnp.exp2((scores[pair, :, cols] - top) * EXP_SCALE)
                total = total + (e[:, :128] + e[:, 128:])
                out = jnp.dot(e.astype(bf16), pair_rows(1, pair, zs, g), preferred_element_type=f32)
                acc = [acc[0] + out[:CUBE, :HEAD_DIM], acc[1] + out[CUBE:, HEAD_DIM:]]
        if top is not None:
            mixed = jnp.concatenate(acc, axis=0) / jnp.sum(total, axis=1, keepdims=True) + coarse
            for n in range(2):
                o_ref[2 * pair + n, zs] = mixed[n * CUBE:(n + 1) * CUBE].astype(bf16)
        return jnp.max(peak, axis=1, keepdims=True)

    def o_copy(dx, n, zs):
        xt = (x + dx) % NX
        return remote(
            o_ref.at[xt, zs], relay_ref.at[x, zs], o_send.at[dx, n], o_recv.at[x, zs], z * NX + xt, 2 * y + c
        )

    def pass_copies(n, zs, act):
        def one(cond, kind, core, src, dst):
            def away():
                copy = remote(src, dst, r_send.at[n, kind], r_recv.at[z, c, kind], zs * NX + x, 2 * y + core)
                if act == "start":
                    copy.start()
                else:
                    copy.wait_send()

            stays = (zs == z) & (c == core)
            pl.when(cond & jnp.logical_not(stays))(away)
            if act == "start":
                pl.when(cond & stays)(
                    lambda: pltpu.make_async_copy(src, dst, r_recv.at[z, c, kind]).start()
                )

        col = pl.ds(pl.multiple_of(z % 5 * HEAD_DIM, HEAD_DIM), HEAD_DIM)
        one(z >= 0, 0, z // 5, relay_ref.at[pl.ds(0, 3), zs], a_ref.at[:, c, :, col])
        xcol = pl.ds(pl.multiple_of((3 + z // 4) * HEAD_DIM, HEAD_DIM), HEAD_DIM)
        third = z % 4 - z % 4 // 3
        one(has_extra, 1, 1, relay_ref.at[3, zs], a_ref.at[third, c, :, xcol])

    def pass_on(n):
        zs = target(n)
        for xs in range(3):
            arrived(relay_ref.at[xs, zs], o_recv.at[xs, zs])
        pl.when(has_extra)(lambda: arrived(relay_ref.at[3, zs], o_recv.at[3, zs]))
        pass_copies(n, zs, "start")

    def step(n, top):
        zs = target(n)
        top = blend(0, zs, top, 1, zs)
        top = blend(1, zs, top, 0, target(jnp.minimum(n + 1, NZ - 1)))

        @pl.when(member)
        def _():
            pltpu.make_async_copy(o_ref.at[x, zs], relay_ref.at[x, zs], o_recv.at[x, zs]).start()
            for dx in XORDER:
                o_copy(dx, n, zs).start()

        pl.when(n >= LAG)(lambda: pass_on(n - LAG))
        return top

    lax.fori_loop(0, NZ, step, blend(None, None, None, 0, target(0)))
    for n in range(NZ - LAG, NZ):
        pass_on(n)

    for zs in range(NZ):
        for cc in range(2):
            col = pl.ds(zs % 5 * HEAD_DIM, HEAD_DIM)
            pl.when(c == zs // 5)(lambda: arrived(a_ref.at[:, cc, :, col], r_recv.at[zs, cc, 0]))
            if zs % 4 != 3:
                xcol = pl.ds((3 + zs // 4) * HEAD_DIM, HEAD_DIM)
                pl.when(c == 1)(lambda: arrived(a_ref.at[zs % 4, cc, :, xcol], r_recv.at[zs, cc, 1]))

    mixed = a_ref[...].reshape(ROWS, FEATS).astype(f32)
    att[c] = (jax.nn.sigmoid(gate_ref[...].astype(f32)) * mixed).astype(bf16)
    att_away = remote(att.at[c], att.at[c], t_sem.at[0], t_sem.at[1], here, sibling)
    att_away.start()
    w_own.wait()
    arrived(weight.at[block(1 - c)], w_sem.at[2])
    arrived(att.at[1 - c], t_sem.at[1])

    def product(band, t):
        rows = pl.ds(pl.multiple_of(band * BAND, BAND), BAND)
        cols = slice(t * TILE, (t + 1) * TILE)
        total = jnp.dot(att[0, rows, :], weight[:FEATS, cols], preferred_element_type=f32)
        return total + jnp.dot(att[1, rows, :], weight[FEATS:, cols], preferred_element_type=f32)

    right, left = (y + 1) % NY, (y + 3) % NY

    def across(t):
        return remote(
            part.at[1, t], passed.at[t], part_send.at[1, t], passed_recv.at[t],
            here, 2 * (right if t < 2 else left) + c,
        )

    def onward(side, t):
        return remote(
            part.at[2 * side, t], landed.at[side, t], part_send.at[2 * side, t], landed_recv.at[side, t],
            here, 2 * (left if side else right) + c,
        )

    for t in (0, 2, 1, 3):
        part[1, t] = product((y + 2) % NY, t).astype(bf16)
        across(t).start()
    for side, t in ((0, 2), (1, 0), (0, 3), (1, 1)):
        part[2 * side, t] = product(left if side else right, t).astype(bf16)
        onward(side, t).start()
    for side, t in ((0, 0), (1, 2), (0, 1), (1, 3)):
        total = product(left if side else right, t)
        arrived(passed.at[t], passed_recv.at[t])
        part[2 * side, t] = (total + passed[t].astype(f32)).astype(bf16)
        onward(side, t).start()

    def rows_of(core):
        return pl.ds(pl.multiple_of(core * BAND_CORE, BAND_CORE), BAND_CORE)

    def columns(core, t):
        return pl.ds(pl.multiple_of(core * COLS + t * TILE, TILE), TILE)

    def give(t):
        return remote(
            done.at[t, rows_of(1 - c)], out_ref.at[:, columns(c, t)],
            done_send.at[0, t], done_recv.at[t], here, 2 * y + 1 - c,
        )

    def keep(t):
        return pltpu.make_async_copy(done.at[t, rows_of(c)], out_ref.at[:, columns(c, t)], done_send.at[1, t])

    for t in (2, 0, 3, 1):
        total = product(y, t)
        for side in range(2):
            arrived(landed.at[side, t], landed_recv.at[side, t])
            total = total + landed[side, t].astype(f32)
        done[t] = total.astype(bf16)
        give(t).start()
        keep(t).start()

    for t in range(TILES):
        give(t).wait_send()
        keep(t).wait()
        arrived(out_ref.at[:, columns(1 - c, t)], done_recv.at[t])
        across(t).wait_send()
        for side in range(2):
            onward(side, t).wait_send()
    w_away.wait_send()
    att_away.wait_send()

    @pl.when(member)
    def _():
        for n in range(NZ):
            for dx in XORDER:
                o_copy(dx, n, target(n)).wait_send()
        for xs in range(NX):
            for zs in range(NZ):
                core_copy(xs, zs).wait_send()

    for n in range(NZ):
        pass_copies(n, target(n), "wait")
    for dx in range(1, NX):
        sel_x(dx).wait_send()
    for n, dz in enumerate(ORDER):
        if dz:
            sel_z(n, dz).wait_send()
    z_copies("wait")
    for n, dz in enumerate(ORDER):
        x_copies(n, (z + dz) % NZ, "wait")
    xq_copies("wait")


def body(query_states, key_states, value_states, gate_states, selection, out_weight):
    bf16 = jnp.bfloat16
    any_spec = pl.BlockSpec(memory_space=pl.ANY)
    dma, vmem = pltpu.SemaphoreType.DMA, pltpu.VMEM
    owner = selection // CUBE_DEV
    places = (owner % NX * NZ + owner // NX) * CUBE_DEV + selection % CUBE_DEV
    places = jnp.pad(places, ((0, 8 - CUBE_DEV), (0, 128 - TOPK)))
    cubes = vmem((NX, NZ, CUBE, HEAD_DIM), bf16)
    return pl.pallas_call(
        kernel,
        out_shape=jax.ShapeDtypeStruct((BAND_CORE, 2 * COLS), bf16),
        in_specs=[any_spec] * 4 + [pl.BlockSpec(memory_space=pltpu.VMEM), any_spec],
        out_specs=any_spec,
        scratch_shapes=[
            vmem((2, 5 * NZ * CUBE_DEV, CUBE, HEAD_DIM), bf16),
            cubes,
            cubes,
            vmem((NX, NZ, 8, 128), jnp.int32),
            pltpu.SMEM((NX, NZ, 8, 128), jnp.int32),
            vmem((2, N_CUBES, HEAD_DIM), bf16),
            vmem((2, 2 * CUBE, TOPK * CUBE), jnp.float32),
            cubes,
            cubes,
            vmem((3, 2, CUBE, FEATS), bf16),
            vmem((2, ROWS, FEATS), bf16),
            vmem((2 * FEATS, COLS), bf16),
            vmem((3, TILES, BAND, TILE), bf16),
            vmem((TILES, BAND, TILE), bf16),
            vmem((2, TILES, BAND, TILE), bf16),
            vmem((TILES, BAND, TILE), bf16),
            dma((NZ, 2, 4)), dma((NZ, 4)),
            dma((NX, NZ)), dma((NX, NZ)),
            dma((NX,)), dma((NX,)),
            dma((NX, NZ)), dma((NX, NZ)),
            dma((NZ,)), dma((NZ,)), dma((NX,)), dma((NX,)), dma,
            dma((NX, NZ)), dma((NX, NZ)), dma((NZ, 2)), dma((NZ, 2, 2)), dma((3,)), dma((2,)),
            dma((3, TILES)), dma((TILES,)), dma((2, TILES)), dma((2, TILES)), dma((TILES,)),
        ],
        compiler_params=pltpu.CompilerParams(
            collective_id=0, has_side_effects=True, vmem_limit_bytes=48 * 2**20
        ),
        name="sparse_attention",
    )(
        places,
        query_states.reshape(3, 2, CUBE, FEATS),
        key_states.reshape(CUBE_DEV, CUBE, FEATS),
        value_states.reshape(CUBE_DEV, CUBE, FEATS),
        gate_states,
        out_weight,
    )


def solution(mesh):
    placed = (
        P("seq", "head"),
        P("seq", "head"),
        P("seq", "head"),
        P("seq", "head"),
        P("seq", None),
        P("head", None),
    )
    return jax.shard_map(
        body, mesh=mesh, in_specs=placed, out_specs=P(("seq", "head"), None), check_vma=False
    )
```

```python
import functools
import math

import jax
import jax.numpy as jnp
from jax import lax
from jax.experimental import pallas as pl
from jax.experimental.pallas import tpu as pltpu
from jax.sharding import PartitionSpec as P

MESH = pl.DeviceIdType.MESH
HEAD_DIM = 128
CUBE = 64
CUBE_DEV = 6
TOPK = 32
NZ, NX = 8, 4
ROWS = CUBE * CUBE_DEV
HEADS_DEV = 5
NY = 4
ORDER = (0, 1, 7, 2, 6, 3, 5, 4)
XORDER = (1, 3, 2)
FEATS = HEADS_DEV * HEAD_DIM
BAND = ROWS // NY
BAND_CORE = BAND // 2
COLS = 2560
TILE = 640
TILES = COLS // TILE
N_CUBES = NZ * NX * CUBE_DEV
GROUP = 4
WIDTH = GROUP * CUBE
LAG = 2
ROUNDS = ((0,), (1, 7), (2, 6), (3, 5), (4,))
CONTRACT_LAST = (((1,), (1,)), ((), ()))
EXP_SCALE = HEAD_DIM ** (-0.5) * math.log2(math.e)


def place():
    seq, head = lax.axis_index("seq"), lax.axis_index("head")
    return seq // NX, seq % NX, head // 2, head % 2


def remote(src, dst, send_sem, recv_sem, seq, head):
    return pltpu.make_async_remote_copy(
        src_ref=src,
        dst_ref=dst,
        send_sem=send_sem,
        recv_sem=recv_sem,
        device_id={"seq": seq, "head": head},
        device_id_type=MESH,
    )


def arrived(ref, sem):
    pltpu.make_async_copy(ref, ref, sem).wait()


def greet(z, x, y, c):
    barrier = pltpu.get_barrier_semaphore()
    for dz in range(NZ):
        for dc in range(2):
            if dz or dc:
                pl.semaphore_signal(
                    barrier,
                    inc=1,
                    device_id={"seq": (z + dz) % NZ * NX + x, "head": 2 * y + (c + dc) % 2},
                    device_id_type=MESH,
                )
    for dx in range(1, NX):
        pl.semaphore_signal(
            barrier,
            inc=1,
            device_id={"seq": z * NX + (x + dx) % NX, "head": 2 * y + c},
            device_id_type=MESH,
        )
    for dy in (1, 3):
        pl.semaphore_signal(
            barrier,
            inc=1,
            device_id={"seq": z * NX + x, "head": 2 * ((y + dy) % NY) + c},
            device_id_type=MESH,
        )
    pl.semaphore_wait(barrier, 2 * NZ - 1 + NX - 1 + 2)


def kernel(
    sel_ref, q_ref, k_ref, v_ref, gate_ref, w_ref, out_ref,
    kv_ref, qr_ref, qf_ref, all_sel_ref, sel, pooled, scores, coarse_scores, o_ref,
    relay_ref, a_ref, att, weight, part, passed, landed, done,
    z_send, z_recv, x_send, x_recv, xq_send, xq_recv, c_send, c_recv,
    sz_send, sz_recv, sx_send, sx_recv, pick_sem,
    o_send, o_recv, r_send, r_recv, w_sem, t_send, t_recv,
    part_send, passed_recv, landed_recv, done_send, done_recv,
):
    f32, bf16 = jnp.float32, jnp.bfloat16
    z, x, y, c = place()
    here = z * NX + x
    sibling = 2 * y + 1 - c
    main_slot = x + x // 3
    extra_slot = 4 - x // 3
    has_extra = z % 4 != 3
    member = (x != 3) | has_extra
    greet(z, x, y, c)

    def tile_at(which, slot, zs):
        return kv_ref.at[which, pl.ds((slot * NZ + zs) * CUBE_DEV, CUBE_DEV)]

    def half(core):
        return pl.ds(pl.multiple_of(core * COLS, COLS), COLS)

    def block(core):
        return pl.ds(pl.multiple_of(core * FEATS, FEATS), FEATS)

    w_own = pltpu.make_async_copy(w_ref.at[:, half(c)], weight.at[block(c)], w_sem.at[0])
    w_away = remote(w_ref.at[:, half(1 - c)], weight.at[block(c)], w_sem.at[1], w_sem.at[2], here, sibling)

    def sel_z(n, dz):
        return remote(
            sel_ref, all_sel_ref.at[x, z], sz_send.at[n], sz_recv.at[z], (z + dz) % NZ * NX + x, 2 * y + c
        )

    def sel_x(dx):
        return remote(
            all_sel_ref.at[x], all_sel_ref.at[x], sx_send.at[dx], sx_recv.at[x], z * NX + (x + dx) % NX, 2 * y + c
        )

    pltpu.make_async_copy(sel_ref, all_sel_ref.at[x, z], sz_recv.at[z]).start()
    for n, dz in enumerate(ORDER):
        if dz:
            sel_z(n, dz).start()

    def z_copies(act, kinds, dzs):
        for dz in dzs:
            zt = (z + dz) % NZ
            for cc in range(2):
                source = k_ref if cc == 0 else v_ref

                def one(cond, kind, src, dst):
                    def away():
                        copy = remote(
                            src, dst, z_send.at[dz, cc, kind], z_recv.at[z, kind], zt * NX + x, 2 * y + cc
                        )
                        if act == "start":
                            copy.start()
                        else:
                            copy.wait_send()

                    if dz:
                        pl.when(cond)(away)
                    else:
                        pl.when(cond & (c != cc))(away)
                        if act == "start":
                            pl.when(cond & (c == cc))(
                                lambda: pltpu.make_async_copy(src, dst, z_recv.at[z, kind]).start()
                            )

                is_main = c == zt // 5
                col = pl.ds(pl.multiple_of(zt % 5 * HEAD_DIM, HEAD_DIM), HEAD_DIM)
                is_extra = (c == 1) & (zt % 4 != 3)
                xcol = pl.ds(pl.multiple_of((3 + zt // 4) * HEAD_DIM, HEAD_DIM), HEAD_DIM)
                rank = zt % 4 - zt % 4 // 3
                if 0 in kinds:
                    one(is_main, 0, source.at[:, :, col], tile_at(cc, main_slot, z))
                    one(is_extra, 1, source.at[:, :, xcol], tile_at(cc, extra_slot, z))
                if 2 in kinds:
                    one(is_main, 2, q_ref.at[:, cc, :, col], qr_ref.at[pl.ds(0, 3), z])
                    one(is_extra, 3, q_ref.at[rank, cc, :, xcol], qr_ref.at[3, z])

    tiles, queries = (0, 1), (2, 3)
    for r in range(2):
        z_copies("start", tiles, ROUNDS[r])
    w_own.start()
    def x_copies(dz, act, kind):
        zs = (z + dz) % NZ
        for dx in XORDER:
            xt = (x + dx) % NX
            slot = main_slot if kind == 0 else 4

            def away():
                copy = remote(
                    tile_at(c, slot, zs), tile_at(c, x, zs),
                    x_send.at[dx, dz], x_recv.at[x, zs], z * NX + xt, 2 * y + c,
                )
                if act == "start":
                    copy.start()
                else:
                    copy.wait_send()

            pl.when(xt != 3 if kind == 0 else (xt == 3) & has_extra)(away)

    def core_copy(xs, zs):
        return remote(
            tile_at(c, xs, zs), tile_at(c, xs, zs),
            c_send.at[xs, zs], c_recv.at[xs, zs], here, sibling,
        )

    def take_x(zs):
        for dx in XORDER:
            xs = (x + dx) % NX

            @pl.when(member)
            def _():
                arrived(tile_at(c, xs, zs), x_recv.at[xs, zs])
                core_copy(xs, zs).start()

    for r, dzs in enumerate(ROUNDS):
        for dz in dzs:
            zs = (z + dz) % NZ
            arrived(tile_at(c, main_slot, zs), z_recv.at[zs, 0])
            x_copies(dz, "start", 0)
            pl.when(x != 3)(lambda: core_copy(x, zs).start())
        if r == 1:
            z_copies("start", tiles, ROUNDS[2])
        if r == 3:
            z_copies("start", tiles, ROUNDS[4])
        if r == 2:
            z_copies("start", tiles, ROUNDS[3])
            for n in range(3):
                z_copies("start", queries, ROUNDS[n])
        if r == 3:
            for n in range(3, 5):
                z_copies("start", queries, ROUNDS[n])
        for dz in dzs:
            zs = (z + dz) % NZ
            pl.when(has_extra)(lambda: arrived(tile_at(c, extra_slot, zs), z_recv.at[zs, 1]))
            x_copies(dz, "start", 1)
            pl.when((x == 3) & has_extra)(lambda: core_copy(x, zs).start())
        if r == 2:
            for zs in range(NZ):
                arrived(all_sel_ref.at[x, zs], sz_recv.at[zs])
            for dx in range(1, NX):
                sel_x(dx).start()
        if r:
            for dz in ROUNDS[r - 1]:
                take_x((z + dz) % NZ)

    def xq_copies(dz, act):
        zs = (z + dz) % NZ
        for dx in range(NX):
            xt = (x + dx) % NX

            def away():
                src, dst = qr_ref.at[xt, zs], qf_ref.at[x, zs]
                if dx:
                    copy = remote(src, dst, xq_send.at[dx, dz], xq_recv.at[x, zs], z * NX + xt, 2 * y + c)
                    if act == "start":
                        copy.start()
                    else:
                        copy.wait_send()
                elif act == "start":
                    pltpu.make_async_copy(src, dst, xq_recv.at[x, zs]).start()

            pl.when((xt != 3) | has_extra)(away)

    for r, dzs in enumerate(ROUNDS):
        for dz in dzs:
            zs = (z + dz) % NZ
            arrived(qr_ref.at[pl.ds(0, 3), zs], z_recv.at[zs, 2])
            pl.when(has_extra)(lambda: arrived(qr_ref.at[3, zs], z_recv.at[zs, 3]))
            xq_copies(dz, "start")
    for dz in ROUNDS[-1]:
        take_x((z + dz) % NZ)
    w_away.start()

    for dx in range(1, NX):
        arrived(all_sel_ref.at[(x + dx) % NX], sx_recv.at[(x + dx) % NX])
    picks = pltpu.make_async_copy(all_sel_ref, sel, pick_sem)
    picks.start()

    @pl.when(member)
    def _():
        for xs in range(NX):
            for zs in range(NZ):
                arrived(qf_ref.at[xs, zs], xq_recv.at[xs, zs])
        for xs in range(NX):
            for zs in range(NZ):
                arrived(tile_at(1 - c, xs, zs), c_recv.at[xs, zs])

    picks.wait()

    rank = x + x // 3 * (z % 4 - x)
    cube = rank * 2 + c - rank // 3 * 2

    def pool(i, _):
        for which in range(2):
            block_of = kv_ref[which, pl.ds(i * 16, 16)].astype(f32)
            sums = jnp.sum(block_of, axis=1)
            pooled[which, pl.ds(pl.multiple_of(i * 16, 16), 16), :] = (sums * (1.0 / CUBE)).astype(bf16)
        return 0

    lax.fori_loop(0, N_CUBES // 16, pool, 0)

    def target(n):
        return (z + 4 + (1 - n % 2 * 2) * ((n + 1) // 2)) % NZ

    def rows(which, xs, zs, g):
        tiles = [
            kv_ref[which, sel[xs, zs, cube, g * GROUP + n]]
            for n in range(GROUP)
        ]
        return jnp.concatenate(tiles, axis=0)

    def pair_rows(which, pair, zs, g):
        return jnp.concatenate([rows(which, 2 * pair, zs, g), rows(which, 2 * pair + 1, zs, g)], axis=1)

    def blend(pair, zs, top, pair_ahead, zs_ahead):
        acc = [jnp.zeros((CUBE, HEAD_DIM), f32) for _ in range(2)]
        total = jnp.zeros((2 * CUBE, 128), f32)
        peak = None
        if top is not None:
            e = jnp.exp2((coarse_scores[pair] - top[1]) * EXP_SCALE)
            coarse = jnp.dot(e.astype(bf16), pooled[1], preferred_element_type=f32)
            coarse = coarse / jnp.sum(e, axis=1, keepdims=True)
        q = [qf_ref[2 * pair_ahead + n, zs_ahead] for n in range(2)]
        s = lax.dot_general(jnp.concatenate(q, axis=0), pooled[0], CONTRACT_LAST, preferred_element_type=f32)
        coarse_scores[pair_ahead] = s
        coarse_peak = jnp.max(s, axis=1, keepdims=True)
        zero = jnp.zeros((CUBE, HEAD_DIM), bf16)
        ahead = jnp.concatenate([
            jnp.concatenate([q[0], zero], axis=1),
            jnp.concatenate([zero, q[1]], axis=1),
        ], axis=0)
        for g in range(TOPK // GROUP):
            cols = slice(g * WIDTH, (g + 1) * WIDTH)
            s = lax.dot_general(ahead, pair_rows(0, pair_ahead, zs_ahead, g), CONTRACT_LAST, preferred_element_type=f32)
            scores[pair_ahead, :, cols] = s
            part_peak = jnp.maximum(s[:, :128], s[:, 128:])
            peak = part_peak if peak is None else jnp.maximum(peak, part_peak)
            if top is not None:
                e = jnp.exp2((scores[pair, :, cols] - top[0]) * EXP_SCALE)
                total = total + (e[:, :128] + e[:, 128:])
                out = jnp.dot(e.astype(bf16), pair_rows(1, pair, zs, g), preferred_element_type=f32)
                acc = [acc[0] + out[:CUBE, :HEAD_DIM], acc[1] + out[CUBE:, HEAD_DIM:]]
        if top is not None:
            mixed = jnp.concatenate(acc, axis=0) / jnp.sum(total, axis=1, keepdims=True) + coarse
            for n in range(2):
                o_ref[2 * pair + n, zs] = mixed[n * CUBE:(n + 1) * CUBE].astype(bf16).reshape(2, CUBE // 2, HEAD_DIM)
        return jnp.max(peak, axis=1, keepdims=True), coarse_peak

    def o_copy(dx, n, zs):
        xt = (x + dx) % NX
        return remote(
            o_ref.at[xt, zs], relay_ref.at[x, zs], o_send.at[dx, n], o_recv.at[x, zs], z * NX + xt, 2 * y + c
        )

    def pass_copies(n, zs, act):
        def one(cond, kind, core, src, dst):
            def away():
                copy = remote(src, dst, r_send.at[n, kind], r_recv.at[z, c, kind], zs * NX + x, 2 * y + core)
                if act == "start":
                    copy.start()
                else:
                    copy.wait_send()

            stays = (zs == z) & (c == core)
            pl.when(cond & jnp.logical_not(stays))(away)
            if act == "start":
                pl.when(cond & stays)(
                    lambda: pltpu.make_async_copy(src, dst, r_recv.at[z, c, kind]).start()
                )

        col = pl.ds(pl.multiple_of(z % 5 * HEAD_DIM, HEAD_DIM), HEAD_DIM)
        one(z >= 0, 0, z // 5, relay_ref.at[pl.ds(0, 3), zs], a_ref.at[:, c, :, :, col])
        xcol = pl.ds(pl.multiple_of((3 + z // 4) * HEAD_DIM, HEAD_DIM), HEAD_DIM)
        third = z % 4 - z % 4 // 3
        one(has_extra, 1, 1, relay_ref.at[3, zs], a_ref.at[third, c, :, :, xcol])

    def pass_on(n):
        zs = target(n)
        for xs in range(3):
            arrived(relay_ref.at[xs, zs], o_recv.at[xs, zs])
        pl.when(has_extra)(lambda: arrived(relay_ref.at[3, zs], o_recv.at[3, zs]))
        pass_copies(n, zs, "start")

    def step(n, top):
        zs = target(n)
        top = blend(0, zs, top, 1, zs)
        top = blend(1, zs, top, 0, target(jnp.minimum(n + 1, NZ - 1)))

        @pl.when(member)
        def _():
            pltpu.make_async_copy(o_ref.at[x, zs], relay_ref.at[x, zs], o_recv.at[x, zs]).start()
            for dx in XORDER:
                o_copy(dx, n, zs).start()

        pl.when(n >= LAG)(lambda: pass_on(n - LAG))
        return top

    lax.fori_loop(0, NZ, step, blend(None, None, None, 0, target(0)))
    for n in range(NZ - LAG, NZ):
        pass_on(n)

    for zs in range(NZ):
        for cc in range(2):
            col = pl.ds(zs % 5 * HEAD_DIM, HEAD_DIM)
            pl.when(c == zs // 5)(lambda: arrived(a_ref.at[:, cc, :, :, col], r_recv.at[zs, cc, 0]))
            if zs % 4 != 3:
                xcol = pl.ds((3 + zs // 4) * HEAD_DIM, HEAD_DIM)
                pl.when(c == 1)(lambda: arrived(a_ref.at[zs % 4, cc, :, :, xcol], r_recv.at[zs, cc, 1]))

    def band_rows(band):
        return pl.ds(pl.multiple_of(band * BAND, BAND), BAND)

    def att_away(n, band):
        return remote(
            att.at[c, band_rows(band)], att.at[c, band_rows(band)], t_send.at[n], t_recv.at[n], here, sibling
        )

    bands = [(y + dy) % NY for dy in (2, 1, 3, 0)]
    for n, band in enumerate(bands):
        for piece in range(3):
            part_of = band * 3 + piece
            mixed = a_ref[part_of // 4, part_of // 2 % 2, part_of % 2].astype(f32)
            gates = jax.nn.sigmoid(gate_ref[part_of].astype(f32))
            start = pl.multiple_of(part_of * (CUBE // 2), CUBE // 2)
            att[c, pl.ds(start, CUBE // 2), :] = (gates * mixed).astype(bf16)
        att_away(n, band).start()
    w_own.wait()
    arrived(weight.at[block(1 - c)], w_sem.at[2])

    def band_here(n):
        arrived(att.at[1 - c, band_rows(bands[n])], t_recv.at[n])

    def product(band, t):
        rows = band_rows(band)
        cols = slice(t * TILE, (t + 1) * TILE)
        total = jnp.dot(att[0, rows, :], weight[:FEATS, cols], preferred_element_type=f32)
        return total + jnp.dot(att[1, rows, :], weight[FEATS:, cols], preferred_element_type=f32)

    right, left = (y + 1) % NY, (y + 3) % NY

    def across(t):
        return remote(
            part.at[1, t], passed.at[t], part_send.at[1, t], passed_recv.at[t],
            here, 2 * (right if t < 2 else left) + c,
        )

    def onward(side, t):
        return remote(
            part.at[2 * side, t], landed.at[side, t], part_send.at[2 * side, t], landed_recv.at[side, t],
            here, 2 * (left if side else right) + c,
        )

    band_here(0)
    for t in (0, 2, 1, 3):
        part[1, t] = product((y + 2) % NY, t).astype(bf16)
        across(t).start()
    band_here(1)
    band_here(2)
    for side, t in ((0, 2), (1, 0), (0, 3), (1, 1)):
        part[2 * side, t] = product(left if side else right, t).astype(bf16)
        onward(side, t).start()
    for side, t in ((0, 0), (1, 2), (0, 1), (1, 3)):
        total = product(left if side else right, t)
        arrived(passed.at[t], passed_recv.at[t])
        part[2 * side, t] = (total + passed[t].astype(f32)).astype(bf16)
        onward(side, t).start()

    def rows_of(core):
        return pl.ds(pl.multiple_of(core * BAND_CORE, BAND_CORE), BAND_CORE)

    def columns(core, t):
        return pl.ds(pl.multiple_of(core * COLS + t * TILE, TILE), TILE)

    def give(t):
        return remote(
            done.at[t, rows_of(1 - c)], out_ref.at[:, columns(c, t)],
            done_send.at[0, t], done_recv.at[t], here, 2 * y + 1 - c,
        )

    def keep(t):
        return pltpu.make_async_copy(done.at[t, rows_of(c)], out_ref.at[:, columns(c, t)], done_send.at[1, t])

    band_here(3)
    for t in (2, 0, 3, 1):
        total = product(y, t)
        for side in range(2):
            arrived(landed.at[side, t], landed_recv.at[side, t])
            total = total + landed[side, t].astype(f32)
        done[t] = total.astype(bf16)
        give(t).start()
        keep(t).start()

    for t in range(TILES):
        give(t).wait_send()
        keep(t).wait()
        arrived(out_ref.at[:, columns(1 - c, t)], done_recv.at[t])
        across(t).wait_send()
        for side in range(2):
            onward(side, t).wait_send()
    w_away.wait_send()
    for n, band in enumerate(bands):
        att_away(n, band).wait_send()

    @pl.when(member)
    def _():
        for n in range(NZ):
            for dx in XORDER:
                o_copy(dx, n, target(n)).wait_send()
        for xs in range(NX):
            for zs in range(NZ):
                core_copy(xs, zs).wait_send()

    for n in range(NZ):
        pass_copies(n, target(n), "wait")
    for dx in range(1, NX):
        sel_x(dx).wait_send()
    for n, dz in enumerate(ORDER):
        if dz:
            sel_z(n, dz).wait_send()
    for dz in range(NZ):
        z_copies("wait", tiles + queries, (dz,))
        x_copies(dz, "wait", 0)
        x_copies(dz, "wait", 1)
        xq_copies(dz, "wait")


def body(query_states, key_states, value_states, gate_states, selection, out_weight):
    bf16 = jnp.bfloat16
    any_spec = pl.BlockSpec(memory_space=pl.ANY)
    dma, vmem = pltpu.SemaphoreType.DMA, pltpu.VMEM
    owner = selection // CUBE_DEV
    places = (owner % NX * NZ + owner // NX) * CUBE_DEV + selection % CUBE_DEV
    places = jnp.pad(places, ((0, 8 - CUBE_DEV), (0, 128 - TOPK)))
    cubes = vmem((NX, NZ, CUBE, HEAD_DIM), bf16)
    halves = vmem((NX, NZ, 2, CUBE // 2, HEAD_DIM), bf16)
    return pl.pallas_call(
        kernel,
        out_shape=jax.ShapeDtypeStruct((BAND_CORE, 2 * COLS), bf16),
        in_specs=[any_spec] * 4 + [pl.BlockSpec(memory_space=pltpu.VMEM), any_spec],
        out_specs=any_spec,
        scratch_shapes=[
            vmem((2, 5 * NZ * CUBE_DEV, CUBE, HEAD_DIM), bf16),
            cubes,
            cubes,
            vmem((NX, NZ, 8, 128), jnp.int32),
            pltpu.SMEM((NX, NZ, 8, 128), jnp.int32),
            vmem((2, N_CUBES, HEAD_DIM), bf16),
            vmem((2, 2 * CUBE, TOPK * CUBE), jnp.float32),
            vmem((2, 2 * CUBE, N_CUBES), jnp.float32),
            halves,
            halves,
            vmem((3, 2, 2, CUBE // 2, FEATS), bf16),
            vmem((2, ROWS, FEATS), bf16),
            vmem((2 * FEATS, COLS), bf16),
            vmem((3, TILES, BAND, TILE), bf16),
            vmem((TILES, BAND, TILE), bf16),
            vmem((2, TILES, BAND, TILE), bf16),
            vmem((TILES, BAND, TILE), bf16),
            dma((NZ, 2, 4)), dma((NZ, 4)),
            dma((NX, NZ)), dma((NX, NZ)),
            dma((NX, NZ)), dma((NX, NZ)),
            dma((NX, NZ)), dma((NX, NZ)),
            dma((NZ,)), dma((NZ,)), dma((NX,)), dma((NX,)), dma,
            dma((NX, NZ)), dma((NX, NZ)), dma((NZ, 2)), dma((NZ, 2, 2)), dma((3,)), dma((NY,)), dma((NY,)),
            dma((3, TILES)), dma((TILES,)), dma((2, TILES)), dma((2, TILES)), dma((TILES,)),
        ],
        compiler_params=pltpu.CompilerParams(
            collective_id=0, has_side_effects=True, vmem_limit_bytes=60 * 2**20
        ),
        name="sparse_attention",
    )(
        places,
        query_states.reshape(3, 2, CUBE, FEATS),
        key_states.reshape(CUBE_DEV, CUBE, FEATS),
        value_states.reshape(CUBE_DEV, CUBE, FEATS),
        gate_states.reshape(2 * CUBE_DEV, CUBE // 2, FEATS),
        out_weight,
    )


def solution(mesh):
    placed = (
        P("seq", "head"),
        P("seq", "head"),
        P("seq", "head"),
        P("seq", "head"),
        P("seq", None),
        P("head", None),
    )
    return jax.shard_map(
        body, mesh=mesh, in_specs=placed, out_specs=P(("seq", "head"), None), check_vma=False
    )
```

```python
import functools
import math

import jax
import jax.numpy as jnp
from jax import lax
from jax.experimental import pallas as pl
from jax.experimental.pallas import tpu as pltpu
from jax.sharding import PartitionSpec as P

MESH = pl.DeviceIdType.MESH
HEAD_DIM = 128
CUBE = 64
CUBE_DEV = 6
TOPK = 32
NZ, NX = 8, 4
ROWS = CUBE * CUBE_DEV
HEADS_DEV = 5
NY = 4
ORDER = (0, 1, 7, 2, 6, 3, 5, 4)
XORDER = (1, 3, 2)
FEATS = HEADS_DEV * HEAD_DIM
BAND = ROWS // NY
BAND_CORE = BAND // 2
COLS = 2560
TILE = 640
TILES = COLS // TILE
N_CUBES = NZ * NX * CUBE_DEV
GROUP = 4
WIDTH = GROUP * CUBE
LAG = 2
ROUNDS = ((0,), (1, 7), (2, 6), (3, 5), (4,))
CONTRACT_LAST = (((1,), (1,)), ((), ()))
EXP_SCALE = HEAD_DIM ** (-0.5) * math.log2(math.e)


def place():
    seq, head = lax.axis_index("seq"), lax.axis_index("head")
    return seq // NX, seq % NX, head // 2, head % 2


def remote(src, dst, send_sem, recv_sem, seq, head):
    return pltpu.make_async_remote_copy(
        src_ref=src,
        dst_ref=dst,
        send_sem=send_sem,
        recv_sem=recv_sem,
        device_id={"seq": seq, "head": head},
        device_id_type=MESH,
    )


def arrived(ref, sem):
    pltpu.make_async_copy(ref, ref, sem).wait()


def greet(z, x, y, c):
    barrier = pltpu.get_barrier_semaphore()
    for dz in range(NZ):
        for dc in range(2):
            if dz or dc:
                pl.semaphore_signal(
                    barrier,
                    inc=1,
                    device_id={"seq": (z + dz) % NZ * NX + x, "head": 2 * y + (c + dc) % 2},
                    device_id_type=MESH,
                )
    for dx in range(1, NX):
        pl.semaphore_signal(
            barrier,
            inc=1,
            device_id={"seq": z * NX + (x + dx) % NX, "head": 2 * y + c},
            device_id_type=MESH,
        )
    for dy in (1, 3):
        pl.semaphore_signal(
            barrier,
            inc=1,
            device_id={"seq": z * NX + x, "head": 2 * ((y + dy) % NY) + c},
            device_id_type=MESH,
        )
    pl.semaphore_wait(barrier, 2 * NZ - 1 + NX - 1 + 2)


def kernel(
    sel_ref, q_ref, k_ref, v_ref, gate_hbm, w_ref, out_ref,
    kv_ref, qr_ref, qf_ref, all_sel_ref, sel, pooled, scores, coarse_scores, o_ref,
    relay_ref, a_ref, gate_ref, att, weight, part, passed, landed, done,
    z_send, z_recv, x_send, x_recv, xq_send, xq_recv, c_send, c_recv,
    sz_send, sz_recv, sx_send, sx_recv, pick_sem,
    o_send, o_recv, r_send, r_recv, gate_sem, w_sem, t_send, t_recv,
    part_send, passed_recv, landed_recv, done_send, done_recv,
):
    f32, bf16 = jnp.float32, jnp.bfloat16
    z, x, y, c = place()
    here = z * NX + x
    sibling = 2 * y + 1 - c
    main_slot = x + x // 3
    extra_slot = 4 - x // 3
    has_extra = z % 4 != 3
    member = (x != 3) | has_extra
    greet(z, x, y, c)

    def tile_at(which, slot, zs):
        return kv_ref.at[which, pl.ds((slot * NZ + zs) * CUBE_DEV, CUBE_DEV)]

    def half(core):
        return pl.ds(pl.multiple_of(core * COLS, COLS), COLS)

    def block(core):
        return pl.ds(pl.multiple_of(core * FEATS, FEATS), FEATS)

    w_own = pltpu.make_async_copy(w_ref.at[:, half(c)], weight.at[block(c)], w_sem.at[0])
    w_away = remote(w_ref.at[:, half(1 - c)], weight.at[block(c)], w_sem.at[1], w_sem.at[2], here, sibling)

    def sel_z(n, dz):
        return remote(
            sel_ref, all_sel_ref.at[x, z], sz_send, sz_recv, (z + dz) % NZ * NX + x, 2 * y + c
        )

    def sel_x(dx):
        return remote(
            all_sel_ref.at[x], all_sel_ref.at[x], sx_send, sx_recv, z * NX + (x + dx) % NX, 2 * y + c
        )

    pltpu.make_async_copy(sel_ref, all_sel_ref.at[x, z], sz_recv).start()
    for n, dz in enumerate(ORDER):
        if dz:
            sel_z(n, dz).start()

    def z_copies(act, kinds, dzs):
        for dz in dzs:
            zt = (z + dz) % NZ
            for cc in range(2):
                source = k_ref if cc == 0 else v_ref

                def one(cond, kind, src, dst):
                    def away():
                        copy = remote(
                            src, dst, z_send.at[dz, cc, kind], z_recv.at[z, kind], zt * NX + x, 2 * y + cc
                        )
                        if act == "start":
                            copy.start()
                        else:
                            copy.wait_send()

                    if dz:
                        pl.when(cond)(away)
                    else:
                        pl.when(cond & (c != cc))(away)
                        if act == "start":
                            pl.when(cond & (c == cc))(
                                lambda: pltpu.make_async_copy(src, dst, z_recv.at[z, kind]).start()
                            )

                is_main = c == zt // 5
                col = pl.ds(pl.multiple_of(zt % 5 * HEAD_DIM, HEAD_DIM), HEAD_DIM)
                is_extra = (c == 1) & (zt % 4 != 3)
                xcol = pl.ds(pl.multiple_of((3 + zt // 4) * HEAD_DIM, HEAD_DIM), HEAD_DIM)
                rank = zt % 4 - zt % 4 // 3
                if 0 in kinds:
                    one(is_main, 0, source.at[:, :, col], tile_at(cc, main_slot, z))
                    one(is_extra, 1, source.at[:, :, xcol], tile_at(cc, extra_slot, z))
                if 2 in kinds:
                    one(is_main, 2, q_ref.at[:, cc, :, col], qr_ref.at[pl.ds(0, 3), z])
                    one(is_extra, 3, q_ref.at[rank, cc, :, xcol], qr_ref.at[3, z])

    tiles, queries = (0, 1), (2, 3)
    for r in range(2):
        z_copies("start", tiles, ROUNDS[r])
    w_own.start()
    gate_in = pltpu.make_async_copy(gate_hbm, gate_ref, gate_sem)
    gate_in.start()
    def x_copies(dz, act, kind):
        zs = (z + dz) % NZ
        for dx in XORDER:
            xt = (x + dx) % NX
            slot = main_slot if kind == 0 else 4

            def away():
                copy = remote(
                    tile_at(c, slot, zs), tile_at(c, x, zs),
                    x_send, x_recv.at[zs], z * NX + xt, 2 * y + c,
                )
                if act == "start":
                    copy.start()
                else:
                    copy.wait_send()

            pl.when(xt != 3 if kind == 0 else (xt == 3) & has_extra)(away)

    def core_copy(xs, zs):
        return remote(
            tile_at(c, xs, zs), tile_at(c, xs, zs),
            c_send, c_recv, here, sibling,
        )

    def take_x(zs):
        pl.when(member)(lambda: arrived(kv_ref.at[c, pl.ds(0, 3 * CUBE_DEV)], x_recv.at[zs]))
        for dx in XORDER:
            xs = (x + dx) % NX

            @pl.when(member)
            def _():
                core_copy(xs, zs).start()

    for r, dzs in enumerate(ROUNDS):
        for dz in dzs:
            zs = (z + dz) % NZ
            arrived(tile_at(c, main_slot, zs), z_recv.at[zs, 0])
            x_copies(dz, "start", 0)
            pl.when(x != 3)(lambda: core_copy(x, zs).start())
        if r == 1:
            z_copies("start", tiles, ROUNDS[2])
        if r == 3:
            z_copies("start", tiles, ROUNDS[4])
        if r == 2:
            z_copies("start", tiles, ROUNDS[3])
            for n in range(3):
                z_copies("start", queries, ROUNDS[n])
        if r == 3:
            for n in range(3, 5):
                z_copies("start", queries, ROUNDS[n])
        for dz in dzs:
            zs = (z + dz) % NZ
            pl.when(has_extra)(lambda: arrived(tile_at(c, extra_slot, zs), z_recv.at[zs, 1]))
            x_copies(dz, "start", 1)
            pl.when((x == 3) & has_extra)(lambda: core_copy(x, zs).start())
        if r == 2:
            arrived(all_sel_ref.at[x], sz_recv)
            for dx in range(1, NX):
                sel_x(dx).start()
        if r:
            for dz in ROUNDS[r - 1]:
                take_x((z + dz) % NZ)

    def xq_copies(dz, act):
        zs = (z + dz) % NZ
        for dx in range(NX):
            xt = (x + dx) % NX

            def away():
                src, dst = qr_ref.at[xt, zs], qf_ref.at[x, zs]
                if dx:
                    copy = remote(src, dst, xq_send, xq_recv, z * NX + xt, 2 * y + c)
                    if act == "start":
                        copy.start()
                    else:
                        copy.wait_send()
                elif act == "start":
                    pltpu.make_async_copy(src, dst, xq_recv).start()

            pl.when((xt != 3) | has_extra)(away)

    arrived(all_sel_ref.at[pl.ds(0, NX - 1)], sx_recv)
    picks = pltpu.make_async_copy(all_sel_ref, sel, pick_sem)
    picks.start()

    for r, dzs in enumerate(ROUNDS):
        for dz in dzs:
            zs = (z + dz) % NZ
            arrived(qr_ref.at[pl.ds(0, 3), zs], z_recv.at[zs, 2])
            pl.when(has_extra)(lambda: arrived(qr_ref.at[3, zs], z_recv.at[zs, 3]))
            xq_copies(dz, "start")
    for dz in ROUNDS[-1]:
        take_x((z + dz) % NZ)
    w_away.start()

    @pl.when(member)
    def _():
        arrived(qf_ref, xq_recv)
        arrived(kv_ref.at[1 - c, pl.ds(0, N_CUBES)], c_recv)

    picks.wait()

    rank = x + x // 3 * (z % 4 - x)
    cube = rank * 2 + c - rank // 3 * 2

    def pool(i, _):
        for which in range(2):
            block_of = kv_ref[which, pl.ds(i * 16, 16)].astype(f32)
            sums = jnp.sum(block_of, axis=1)
            pooled[which, pl.ds(pl.multiple_of(i * 16, 16), 16), :] = (sums * (1.0 / CUBE)).astype(bf16)
        return 0

    lax.fori_loop(0, N_CUBES // 16, pool, 0)

    def target(n):
        return (z + 4 + (1 - n % 2 * 2) * ((n + 1) // 2)) % NZ

    def rows(which, xs, zs, g):
        tiles = [
            kv_ref[which, sel[xs, zs, cube, g * GROUP + n]]
            for n in range(GROUP)
        ]
        return jnp.concatenate(tiles, axis=0)

    def pair_rows(which, pair, zs, g):
        return jnp.concatenate([rows(which, 2 * pair, zs, g), rows(which, 2 * pair + 1, zs, g)], axis=1)

    def blend(pair, zs, top, pair_ahead, zs_ahead):
        acc = [jnp.zeros((CUBE, HEAD_DIM), f32) for _ in range(2)]
        total = jnp.zeros((2 * CUBE, 128), f32)
        peak = None
        if top is not None:
            e = jnp.exp2((coarse_scores[pair] - top[1]) * EXP_SCALE)
            coarse = jnp.dot(e.astype(bf16), pooled[1], preferred_element_type=f32)
            coarse = coarse / jnp.sum(e, axis=1, keepdims=True)
        q = [qf_ref[2 * pair_ahead + n, zs_ahead] for n in range(2)]
        s = lax.dot_general(jnp.concatenate(q, axis=0), pooled[0], CONTRACT_LAST, preferred_element_type=f32)
        coarse_scores[pair_ahead] = s
        coarse_peak = jnp.max(s, axis=1, keepdims=True)
        zero = jnp.zeros((CUBE, HEAD_DIM), bf16)
        ahead = jnp.concatenate([
            jnp.concatenate([q[0], zero], axis=1),
            jnp.concatenate([zero, q[1]], axis=1),
        ], axis=0)
        for g in range(TOPK // GROUP):
            cols = slice(g * WIDTH, (g + 1) * WIDTH)
            s = lax.dot_general(ahead, pair_rows(0, pair_ahead, zs_ahead, g), CONTRACT_LAST, preferred_element_type=f32)
            scores[pair_ahead, :, cols] = s
            part_peak = jnp.maximum(s[:, :128], s[:, 128:])
            peak = part_peak if peak is None else jnp.maximum(peak, part_peak)
            if top is not None:
                e = jnp.exp2((scores[pair, :, cols] - top[0]) * EXP_SCALE)
                total = total + (e[:, :128] + e[:, 128:])
                out = jnp.dot(e.astype(bf16), pair_rows(1, pair, zs, g), preferred_element_type=f32)
                acc = [acc[0] + out[:CUBE, :HEAD_DIM], acc[1] + out[CUBE:, HEAD_DIM:]]
        if top is not None:
            mixed = jnp.concatenate(acc, axis=0) / jnp.sum(total, axis=1, keepdims=True) + coarse
            for n in range(2):
                o_ref[2 * pair + n, zs] = mixed[n * CUBE:(n + 1) * CUBE].astype(bf16).reshape(2, CUBE // 2, HEAD_DIM)
        return jnp.max(peak, axis=1, keepdims=True), coarse_peak

    def o_copy(dx, n, zs):
        xt = (x + dx) % NX
        return remote(
            o_ref.at[xt, zs], relay_ref.at[x, zs], o_send, o_recv.at[zs], z * NX + xt, 2 * y + c
        )

    def pass_copies(n, zs, act):
        def one(cond, kind, core, src, dst):
            def away():
                copy = remote(src, dst, r_send.at[n, kind], r_recv, zs * NX + x, 2 * y + core)
                if act == "start":
                    copy.start()
                else:
                    copy.wait_send()

            stays = (zs == z) & (c == core)
            pl.when(cond & jnp.logical_not(stays))(away)
            if act == "start":
                pl.when(cond & stays)(
                    lambda: pltpu.make_async_copy(src, dst, r_recv).start()
                )

        col = pl.ds(pl.multiple_of(z % 5 * HEAD_DIM, HEAD_DIM), HEAD_DIM)
        one(z >= 0, 0, z // 5, relay_ref.at[pl.ds(0, 3), zs], a_ref.at[:, c, :, :, col])
        xcol = pl.ds(pl.multiple_of((3 + z // 4) * HEAD_DIM, HEAD_DIM), HEAD_DIM)
        third = z % 4 - z % 4 // 3
        one(has_extra, 1, 1, relay_ref.at[3, zs], a_ref.at[third, c, :, :, xcol])

    def pass_on(n):
        zs = target(n)
        pl.when(has_extra)(lambda: arrived(relay_ref.at[:, zs], o_recv.at[zs]))
        pl.when(jnp.logical_not(has_extra))(lambda: arrived(relay_ref.at[pl.ds(0, 3), zs], o_recv.at[zs]))
        pass_copies(n, zs, "start")

    def step(n, top):
        zs = target(n)
        top = blend(0, zs, top, 1, zs)
        top = blend(1, zs, top, 0, target(jnp.minimum(n + 1, NZ - 1)))

        @pl.when(member)
        def _():
            pltpu.make_async_copy(o_ref.at[x, zs], relay_ref.at[x, zs], o_recv.at[zs]).start()
            for dx in XORDER:
                o_copy(dx, n, zs).start()

        pl.when(n >= LAG)(lambda: pass_on(n - LAG))
        return top

    lax.fori_loop(0, NZ, step, blend(None, None, None, 0, target(0)))
    for n in range(NZ - LAG, NZ):
        pass_on(n)

    gate_in.wait()
    arrived(a_ref, r_recv)

    def band_rows(band):
        return pl.ds(pl.multiple_of(band * BAND, BAND), BAND)

    def att_away(n, band):
        return remote(
            att.at[c, band_rows(band)], att.at[c, band_rows(band)], t_send, t_recv.at[n], here, sibling
        )

    bands = [(y + dy) % NY for dy in (2, 1, 3, 0)]
    for n, band in enumerate(bands):
        for piece in range(3):
            part_of = band * 3 + piece
            mixed = a_ref[part_of // 4, part_of // 2 % 2, part_of % 2].astype(f32)
            gates = jax.nn.sigmoid(gate_ref[part_of].astype(f32))
            start = pl.multiple_of(part_of * (CUBE // 2), CUBE // 2)
            att[c, pl.ds(start, CUBE // 2), :] = (gates * mixed).astype(bf16)
        att_away(n, band).start()
    w_own.wait()
    arrived(weight.at[block(1 - c)], w_sem.at[2])

    def band_here(n):
        arrived(att.at[1 - c, band_rows(bands[n])], t_recv.at[n])

    def product(band, t):
        rows = band_rows(band)
        cols = slice(t * TILE, (t + 1) * TILE)
        total = jnp.dot(att[0, rows, :], weight[:FEATS, cols], preferred_element_type=f32)
        return total + jnp.dot(att[1, rows, :], weight[FEATS:, cols], preferred_element_type=f32)

    right, left = (y + 1) % NY, (y + 3) % NY

    def across(t):
        return remote(
            part.at[1, t], passed.at[t], part_send.at[0], passed_recv.at[t],
            here, 2 * (right if t < 2 else left) + c,
        )

    def onward(side, t):
        return remote(
            part.at[2 * side, t], landed.at[side, t], part_send.at[1], landed_recv.at[side, t],
            here, 2 * (left if side else right) + c,
        )

    band_here(0)
    for t in (0, 2, 1, 3):
        part[1, t] = product((y + 2) % NY, t).astype(bf16)
        across(t).start()
    band_here(1)
    band_here(2)
    for side, t in ((0, 2), (1, 0), (0, 3), (1, 1)):
        part[2 * side, t] = product(left if side else right, t).astype(bf16)
        onward(side, t).start()
    @pl.when(member)
    def _():
        arrived(o_ref.at[pl.ds(0, 3)], o_send)
        arrived(kv_ref.at[c, pl.ds(0, N_CUBES)], c_send)

    for n in range(NZ):
        pass_copies(n, target(n), "wait")
    arrived(all_sel_ref.at[pl.ds(0, NX - 1)], sx_send)
    arrived(all_sel_ref.at[x, pl.ds(0, NZ - 1)], sz_send)
    for dz in range(NZ):
        z_copies("wait", tiles + queries, (dz,))

    to_three = (x == 3) | has_extra

    @pl.when(to_three)
    def _():
        arrived(kv_ref.at[c, pl.ds(0, 3 * NZ * CUBE_DEV)], x_send)
        arrived(qf_ref.at[pl.ds(0, 3)], xq_send)

    @pl.when(jnp.logical_not(to_three))
    def _():
        arrived(kv_ref.at[c, pl.ds(0, 2 * NZ * CUBE_DEV)], x_send)
        arrived(qf_ref.at[pl.ds(0, 2)], xq_send)

    for side, t in ((0, 0), (1, 2), (0, 1), (1, 3)):
        total = product(left if side else right, t)
        arrived(passed.at[t], passed_recv.at[t])
        part[2 * side, t] = (total + passed[t].astype(f32)).astype(bf16)
        onward(side, t).start()

    def rows_of(core):
        return pl.ds(pl.multiple_of(core * BAND_CORE, BAND_CORE), BAND_CORE)

    def columns(core, t):
        return pl.ds(pl.multiple_of(core * COLS + t * TILE, TILE), TILE)

    def give(t):
        return remote(
            done.at[t, rows_of(1 - c)], out_ref.at[:, columns(c, t)],
            done_send.at[0], done_recv, here, 2 * y + 1 - c,
        )

    def keep(t):
        return pltpu.make_async_copy(done.at[t, rows_of(c)], out_ref.at[:, columns(c, t)], done_send.at[1])

    band_here(3)
    for t in (2, 0, 3, 1):
        total = product(y, t)
        for side in range(2):
            arrived(landed.at[side, t], landed_recv.at[side, t])
            total = total + landed[side, t].astype(f32)
        done[t] = total.astype(bf16)
        give(t).start()
        keep(t).start()

    arrived(passed, part_send.at[0])
    arrived(landed, part_send.at[1])
    arrived(out_ref.at[:, half(c)], done_send.at[0])
    arrived(out_ref.at[:, half(c)], done_send.at[1])
    arrived(out_ref.at[:, half(1 - c)], done_recv)
    w_away.wait_send()
    arrived(att.at[c], t_send)


def body(query_states, key_states, value_states, gate_states, selection, out_weight):
    bf16 = jnp.bfloat16
    any_spec = pl.BlockSpec(memory_space=pl.ANY)
    dma, vmem = pltpu.SemaphoreType.DMA, pltpu.VMEM
    owner = selection // CUBE_DEV
    places = (owner % NX * NZ + owner // NX) * CUBE_DEV + selection % CUBE_DEV
    places = jnp.pad(places, ((0, 8 - CUBE_DEV), (0, 128 - TOPK)))
    cubes = vmem((NX, NZ, CUBE, HEAD_DIM), bf16)
    halves = vmem((NX, NZ, 2, CUBE // 2, HEAD_DIM), bf16)
    return pl.pallas_call(
        kernel,
        out_shape=jax.ShapeDtypeStruct((BAND_CORE, 2 * COLS), bf16),
        in_specs=[any_spec] * 6,
        out_specs=any_spec,
        scratch_shapes=[
            vmem((2, 5 * NZ * CUBE_DEV, CUBE, HEAD_DIM), bf16),
            cubes,
            cubes,
            vmem((NX, NZ, 8, 128), jnp.int32),
            pltpu.SMEM((NX, NZ, 8, 128), jnp.int32),
            vmem((2, N_CUBES, HEAD_DIM), bf16),
            vmem((2, 2 * CUBE, TOPK * CUBE), jnp.float32),
            vmem((2, 2 * CUBE, N_CUBES), jnp.float32),
            halves,
            halves,
            vmem((3, 2, 2, CUBE // 2, FEATS), bf16),
            vmem((2 * CUBE_DEV, CUBE // 2, FEATS), bf16),
            vmem((2, ROWS, FEATS), bf16),
            vmem((2 * FEATS, COLS), bf16),
            vmem((3, TILES, BAND, TILE), bf16),
            vmem((TILES, BAND, TILE), bf16),
            vmem((2, TILES, BAND, TILE), bf16),
            vmem((TILES, BAND, TILE), bf16),
            dma((NZ, 2, 4)), dma((NZ, 4)),
            dma, dma((NZ,)), dma, dma, dma, dma,
            dma, dma, dma, dma, dma,
            dma, dma((NZ,)), dma((NZ, 2)), dma, dma, dma((3,)), dma, dma((NY,)),
            dma((2,)), dma((TILES,)), dma((2, TILES)), dma((2,)), dma,
        ],
        compiler_params=pltpu.CompilerParams(
            collective_id=0, has_side_effects=True, vmem_limit_bytes=60 * 2**20
        ),
        name="sparse_attention",
    )(
        places,
        query_states.reshape(3, 2, CUBE, FEATS),
        key_states.reshape(CUBE_DEV, CUBE, FEATS),
        value_states.reshape(CUBE_DEV, CUBE, FEATS),
        gate_states.reshape(2 * CUBE_DEV, CUBE // 2, FEATS),
        out_weight,
    )


def solution(mesh):
    placed = (
        P("seq", "head"),
        P("seq", "head"),
        P("seq", "head"),
        P("seq", "head"),
        P("seq", None),
        P("head", None),
    )
    return jax.shard_map(
        body, mesh=mesh, in_specs=placed, out_specs=P(("seq", "head"), None), check_vma=False
    )
```

```python
import functools
import math

import jax
import jax.numpy as jnp
from jax import lax
from jax.experimental import pallas as pl
from jax.experimental.pallas import tpu as pltpu
from jax.sharding import PartitionSpec as P

MESH = pl.DeviceIdType.MESH
HEAD_DIM = 128
CUBE = 64
CUBE_DEV = 6
TOPK = 32
NZ, NX = 8, 4
ROWS = CUBE * CUBE_DEV
HEADS_DEV = 5
NY = 4
ORDER = (0, 1, 7, 2, 6, 3, 5, 4)
XORDER = (1, 3, 2)
FEATS = HEADS_DEV * HEAD_DIM
BAND = ROWS // NY
BAND_CORE = BAND // 2
COLS = 2560
TILE = 640
TILES = COLS // TILE
N_CUBES = NZ * NX * CUBE_DEV
GROUP = 4
WIDTH = GROUP * CUBE
LAG = 3
ROUNDS = ((0,), (1, 7), (2, 6), (3, 5), (4,))
CONTRACT_LAST = (((1,), (1,)), ((), ()))
EXP_SCALE = HEAD_DIM ** (-0.5) * math.log2(math.e)


def place():
    seq, head = lax.axis_index("seq"), lax.axis_index("head")
    return seq // NX, seq % NX, head // 2, head % 2


def remote(src, dst, send_sem, recv_sem, seq, head):
    return pltpu.make_async_remote_copy(
        src_ref=src,
        dst_ref=dst,
        send_sem=send_sem,
        recv_sem=recv_sem,
        device_id={"seq": seq, "head": head},
        device_id_type=MESH,
    )


def arrived(ref, sem):
    pltpu.make_async_copy(ref, ref, sem).wait()


def greet(z, x, y, c):
    barrier = pltpu.get_barrier_semaphore()
    for dz in range(NZ):
        for dc in range(2):
            if dz or dc:
                pl.semaphore_signal(
                    barrier,
                    inc=1,
                    device_id={"seq": (z + dz) % NZ * NX + x, "head": 2 * y + (c + dc) % 2},
                    device_id_type=MESH,
                )
    for dx in range(1, NX):
        pl.semaphore_signal(
            barrier,
            inc=1,
            device_id={"seq": z * NX + (x + dx) % NX, "head": 2 * y + c},
            device_id_type=MESH,
        )
    for dy in (1, 3):
        pl.semaphore_signal(
            barrier,
            inc=1,
            device_id={"seq": z * NX + x, "head": 2 * ((y + dy) % NY) + c},
            device_id_type=MESH,
        )
    pl.semaphore_wait(barrier, 2 * NZ - 1 + NX - 1 + 2)


def kernel(
    sel_ref, q_ref, k_ref, v_ref, gate_hbm, w_ref, out_ref,
    kv_ref, qr_ref, qf_ref, all_sel_ref, sel, pooled, scores, coarse_scores, o_ref,
    relay_ref, a_ref, gate_ref, att, weight, part, passed, landed, done,
    z_send, z_recv, x_send, x_recv, xq_send, xq_recv, c_send, c_recv,
    sz_send, sz_recv, sx_send, sx_recv, pick_sem,
    o_send, o_recv, r_send, r_recv, gate_sem, w_sem, t_send, t_recv,
    part_send, passed_recv, landed_recv, done_send, done_recv,
):
    f32, bf16 = jnp.float32, jnp.bfloat16
    z, x, y, c = place()
    here = z * NX + x
    sibling = 2 * y + 1 - c
    main_slot = x + x // 3
    extra_slot = 4 - x // 3
    has_extra = z % 4 != 3
    member = (x != 3) | has_extra
    greet(z, x, y, c)

    def tile_at(which, slot, zs):
        return kv_ref.at[which, pl.ds((slot * NZ + zs) * CUBE_DEV, CUBE_DEV)]

    def half(core):
        return pl.ds(pl.multiple_of(core * COLS, COLS), COLS)

    def block(core):
        return pl.ds(pl.multiple_of(core * FEATS, FEATS), FEATS)

    w_own = pltpu.make_async_copy(w_ref.at[:, half(c)], weight.at[block(c)], w_sem.at[0])
    w_away = remote(w_ref.at[:, half(1 - c)], weight.at[block(c)], w_sem.at[1], w_sem.at[2], here, sibling)

    def sel_z(n, dz):
        return remote(
            sel_ref, all_sel_ref.at[x, z], sz_send, sz_recv, (z + dz) % NZ * NX + x, 2 * y + c
        )

    def sel_x(dx):
        return remote(
            all_sel_ref.at[x], all_sel_ref.at[x], sx_send, sx_recv, z * NX + (x + dx) % NX, 2 * y + c
        )

    pltpu.make_async_copy(sel_ref, all_sel_ref.at[x, z], sz_recv).start()
    for n, dz in enumerate(ORDER):
        if dz:
            sel_z(n, dz).start()

    def z_copies(act, kinds, dzs):
        for dz in dzs:
            zt = (z + dz) % NZ
            for cc in range(2):
                source = k_ref if cc == 0 else v_ref

                def one(cond, kind, src, dst):
                    def away():
                        copy = remote(
                            src, dst, z_send.at[dz, cc, kind], z_recv.at[z, kind], zt * NX + x, 2 * y + cc
                        )
                        if act == "start":
                            copy.start()
                        else:
                            copy.wait_send()

                    if dz:
                        pl.when(cond)(away)
                    else:
                        pl.when(cond & (c != cc))(away)
                        if act == "start":
                            pl.when(cond & (c == cc))(
                                lambda: pltpu.make_async_copy(src, dst, z_recv.at[z, kind]).start()
                            )

                is_main = c == zt // 5
                col = pl.ds(pl.multiple_of(zt % 5 * HEAD_DIM, HEAD_DIM), HEAD_DIM)
                is_extra = (c == 1) & (zt % 4 != 3)
                xcol = pl.ds(pl.multiple_of((3 + zt // 4) * HEAD_DIM, HEAD_DIM), HEAD_DIM)
                rank = zt % 4 - zt % 4 // 3
                if 0 in kinds:
                    one(is_main, 0, source.at[:, :, col], tile_at(cc, main_slot, z))
                    one(is_extra, 1, source.at[:, :, xcol], tile_at(cc, extra_slot, z))
                if 2 in kinds:
                    one(is_main, 2, q_ref.at[:, cc, :, col], qr_ref.at[pl.ds(0, 3), z])
                    one(is_extra, 3, q_ref.at[rank, cc, :, xcol], qr_ref.at[3, z])

    tiles, queries = (0, 1), (2, 3)
    for r in range(2):
        z_copies("start", tiles, ROUNDS[r])
    w_own.start()
    gate_in = pltpu.make_async_copy(gate_hbm, gate_ref, gate_sem)
    gate_in.start()
    def x_copies(dz, act, kind):
        zs = (z + dz) % NZ
        for dx in XORDER:
            xt = (x + dx) % NX
            slot = main_slot if kind == 0 else 4

            def away():
                copy = remote(
                    tile_at(c, slot, zs), tile_at(c, x, zs),
                    x_send, x_recv.at[zs], z * NX + xt, 2 * y + c,
                )
                if act == "start":
                    copy.start()
                else:
                    copy.wait_send()

            pl.when(xt != 3 if kind == 0 else (xt == 3) & has_extra)(away)

    def core_copy(xs, zs):
        return remote(
            tile_at(c, xs, zs), tile_at(c, xs, zs),
            c_send, c_recv, here, sibling,
        )

    def take_x(zs):
        pl.when(member)(lambda: arrived(kv_ref.at[c, pl.ds(0, 3 * CUBE_DEV)], x_recv.at[zs]))
        for dx in XORDER:
            xs = (x + dx) % NX

            @pl.when(member)
            def _():
                core_copy(xs, zs).start()

    for r, dzs in enumerate(ROUNDS):
        for dz in dzs:
            zs = (z + dz) % NZ
            arrived(tile_at(c, main_slot, zs), z_recv.at[zs, 0])
            x_copies(dz, "start", 0)
            pl.when(x != 3)(lambda: core_copy(x, zs).start())
        if r == 1:
            z_copies("start", tiles, ROUNDS[2])
        if r == 3:
            z_copies("start", tiles, ROUNDS[4])
        if r == 2:
            z_copies("start", tiles, ROUNDS[3])
            for n in range(3):
                z_copies("start", queries, ROUNDS[n])
        if r == 3:
            for n in range(3, 5):
                z_copies("start", queries, ROUNDS[n])
        for dz in dzs:
            zs = (z + dz) % NZ
            pl.when(has_extra)(lambda: arrived(tile_at(c, extra_slot, zs), z_recv.at[zs, 1]))
            x_copies(dz, "start", 1)
            pl.when((x == 3) & has_extra)(lambda: core_copy(x, zs).start())
        if r == 2:
            arrived(all_sel_ref.at[x], sz_recv)
            for dx in range(1, NX):
                sel_x(dx).start()
        if r:
            for dz in ROUNDS[r - 1]:
                take_x((z + dz) % NZ)

    def xq_copies(dz, act):
        zs = (z + dz) % NZ
        for dx in range(NX):
            xt = (x + dx) % NX

            def away():
                src, dst = qr_ref.at[xt, zs], qf_ref.at[x, zs]
                if dx:
                    copy = remote(src, dst, xq_send, xq_recv, z * NX + xt, 2 * y + c)
                    if act == "start":
                        copy.start()
                    else:
                        copy.wait_send()
                elif act == "start":
                    pltpu.make_async_copy(src, dst, xq_recv).start()

            pl.when((xt != 3) | has_extra)(away)

    arrived(all_sel_ref.at[pl.ds(0, NX - 1)], sx_recv)
    picks = pltpu.make_async_copy(all_sel_ref, sel, pick_sem)
    picks.start()

    for r, dzs in enumerate(ROUNDS):
        for dz in dzs:
            zs = (z + dz) % NZ
            arrived(qr_ref.at[pl.ds(0, 3), zs], z_recv.at[zs, 2])
            pl.when(has_extra)(lambda: arrived(qr_ref.at[3, zs], z_recv.at[zs, 3]))
            xq_copies(dz, "start")
    for dz in ROUNDS[-1]:
        take_x((z + dz) % NZ)
    w_away.start()

    def pool(which):
        def some(i, _):
            sums = jnp.sum(kv_ref[which, pl.ds(i * 16, 16)].astype(f32), axis=1)
            pooled[which, pl.ds(pl.multiple_of(i * 16, 16), 16), :] = (sums * (1.0 / CUBE)).astype(bf16)
            return 0

        lax.fori_loop(0, N_CUBES // 16, some, 0)

    pool(c)

    @pl.when(member)
    def _():
        arrived(qf_ref, xq_recv)
        arrived(kv_ref.at[1 - c, pl.ds(0, N_CUBES)], c_recv)

    pool(1 - c)
    picks.wait()

    rank = x + x // 3 * (z % 4 - x)
    cube = rank * 2 + c - rank // 3 * 2

    def target(n):
        return (z + 4 + (1 - n % 2 * 2) * ((n + 1) // 2)) % NZ

    def rows(which, xs, zs, g):
        tiles = [
            kv_ref[which, sel[xs, zs, cube, g * GROUP + n]]
            for n in range(GROUP)
        ]
        return jnp.concatenate(tiles, axis=0)

    def pair_rows(which, pair, zs, g):
        return jnp.concatenate([rows(which, 2 * pair, zs, g), rows(which, 2 * pair + 1, zs, g)], axis=1)

    def blend(pair, zs, top, pair_ahead, zs_ahead):
        acc = [jnp.zeros((CUBE, HEAD_DIM), f32) for _ in range(2)]
        total = jnp.zeros((2 * CUBE, 128), f32)
        peak = None
        if top is not None:
            e = jnp.exp2((coarse_scores[pair] - top[1]) * EXP_SCALE)
            coarse = jnp.dot(e.astype(bf16), pooled[1], preferred_element_type=f32)
            coarse = coarse / jnp.sum(e, axis=1, keepdims=True)
        q = [qf_ref[2 * pair_ahead + n, zs_ahead] for n in range(2)]
        s = lax.dot_general(jnp.concatenate(q, axis=0), pooled[0], CONTRACT_LAST, preferred_element_type=f32)
        coarse_scores[pair_ahead] = s
        coarse_peak = jnp.max(s, axis=1, keepdims=True)
        zero = jnp.zeros((CUBE, HEAD_DIM), bf16)
        ahead = jnp.concatenate([
            jnp.concatenate([q[0], zero], axis=1),
            jnp.concatenate([zero, q[1]], axis=1),
        ], axis=0)
        for g in range(TOPK // GROUP):
            cols = slice(g * WIDTH, (g + 1) * WIDTH)
            s = lax.dot_general(ahead, pair_rows(0, pair_ahead, zs_ahead, g), CONTRACT_LAST, preferred_element_type=f32)
            scores[pair_ahead, :, cols] = s
            part_peak = jnp.maximum(s[:, :128], s[:, 128:])
            peak = part_peak if peak is None else jnp.maximum(peak, part_peak)
            if top is not None:
                e = jnp.exp2((scores[pair, :, cols] - top[0]) * EXP_SCALE)
                total = total + (e[:, :128] + e[:, 128:])
                out = jnp.dot(e.astype(bf16), pair_rows(1, pair, zs, g), preferred_element_type=f32)
                acc = [acc[0] + out[:CUBE, :HEAD_DIM], acc[1] + out[CUBE:, HEAD_DIM:]]
        if top is not None:
            mixed = jnp.concatenate(acc, axis=0) / jnp.sum(total, axis=1, keepdims=True) + coarse
            for n in range(2):
                o_ref[2 * pair + n, zs] = mixed[n * CUBE:(n + 1) * CUBE].astype(bf16).reshape(2, CUBE // 2, HEAD_DIM)
        return jnp.max(peak, axis=1, keepdims=True), coarse_peak

    def o_copy(dx, n, zs):
        xt = (x + dx) % NX
        return remote(
            o_ref.at[xt, zs], relay_ref.at[x, zs], o_send, o_recv.at[zs], z * NX + xt, 2 * y + c
        )

    def pass_copies(n, zs, act):
        def one(cond, kind, core, src, dst):
            def away():
                copy = remote(src, dst, r_send.at[n, kind], r_recv, zs * NX + x, 2 * y + core)
                if act == "start":
                    copy.start()
                else:
                    copy.wait_send()

            stays = (zs == z) & (c == core)
            pl.when(cond & jnp.logical_not(stays))(away)
            if act == "start":
                pl.when(cond & stays)(
                    lambda: pltpu.make_async_copy(src, dst, r_recv).start()
                )

        col = pl.ds(pl.multiple_of(z % 5 * HEAD_DIM, HEAD_DIM), HEAD_DIM)
        one(z >= 0, 0, z // 5, relay_ref.at[pl.ds(0, 3), zs], a_ref.at[:, c, :, :, col])
        xcol = pl.ds(pl.multiple_of((3 + z // 4) * HEAD_DIM, HEAD_DIM), HEAD_DIM)
        third = z % 4 - z % 4 // 3
        one(has_extra, 1, 1, relay_ref.at[3, zs], a_ref.at[third, c, :, :, xcol])

    def pass_on(n):
        zs = target(n)
        pl.when(has_extra)(lambda: arrived(relay_ref.at[:, zs], o_recv.at[zs]))
        pl.when(jnp.logical_not(has_extra))(lambda: arrived(relay_ref.at[pl.ds(0, 3), zs], o_recv.at[zs]))
        pass_copies(n, zs, "start")

    def step(n, top):
        zs = target(n)
        top = blend(0, zs, top, 1, zs)
        top = blend(1, zs, top, 0, target(jnp.minimum(n + 1, NZ - 1)))

        @pl.when(member)
        def _():
            pltpu.make_async_copy(o_ref.at[x, zs], relay_ref.at[x, zs], o_recv.at[zs]).start()
            for dx in XORDER:
                o_copy(dx, n, zs).start()

        pl.when(n >= LAG)(lambda: pass_on(n - LAG))
        return top

    lax.fori_loop(0, NZ, step, blend(None, None, None, 0, target(0)))
    for n in range(NZ - LAG, NZ):
        pass_on(n)

    gate_in.wait()
    arrived(a_ref, r_recv)

    def band_rows(band):
        return pl.ds(pl.multiple_of(band * BAND, BAND), BAND)

    def att_away(n, band):
        return remote(
            att.at[c, band_rows(band)], att.at[c, band_rows(band)], t_send, t_recv.at[n], here, sibling
        )

    bands = [(y + dy) % NY for dy in (2, 1, 3, 0)]
    for n, band in enumerate(bands):
        for piece in range(3):
            part_of = band * 3 + piece
            mixed = a_ref[part_of // 4, part_of // 2 % 2, part_of % 2].astype(f32)
            gates = jax.nn.sigmoid(gate_ref[part_of].astype(f32))
            start = pl.multiple_of(part_of * (CUBE // 2), CUBE // 2)
            att[c, pl.ds(start, CUBE // 2), :] = (gates * mixed).astype(bf16)
        att_away(n, band).start()
    w_own.wait()
    arrived(weight.at[block(1 - c)], w_sem.at[2])

    def band_here(n):
        arrived(att.at[1 - c, band_rows(bands[n])], t_recv.at[n])

    def product(band, t):
        rows = band_rows(band)
        cols = slice(t * TILE, (t + 1) * TILE)
        total = jnp.dot(att[0, rows, :], weight[:FEATS, cols], preferred_element_type=f32)
        return total + jnp.dot(att[1, rows, :], weight[FEATS:, cols], preferred_element_type=f32)

    right, left = (y + 1) % NY, (y + 3) % NY

    def across(t):
        return remote(
            part.at[1, t], passed.at[t], part_send.at[0], passed_recv.at[t],
            here, 2 * (right if t < 2 else left) + c,
        )

    def onward(side, t):
        return remote(
            part.at[2 * side, t], landed.at[side, t], part_send.at[1], landed_recv.at[side, t],
            here, 2 * (left if side else right) + c,
        )

    band_here(0)
    for t in (0, 2, 1, 3):
        part[1, t] = product((y + 2) % NY, t).astype(bf16)
        across(t).start()
    band_here(1)
    band_here(2)
    for side, t in ((0, 2), (1, 0), (0, 3), (1, 1)):
        part[2 * side, t] = product(left if side else right, t).astype(bf16)
        onward(side, t).start()
    @pl.when(member)
    def _():
        arrived(o_ref.at[pl.ds(0, 3)], o_send)
        arrived(kv_ref.at[c, pl.ds(0, N_CUBES)], c_send)

    for n in range(NZ):
        pass_copies(n, target(n), "wait")
    arrived(all_sel_ref.at[pl.ds(0, NX - 1)], sx_send)
    arrived(all_sel_ref.at[x, pl.ds(0, NZ - 1)], sz_send)
    for dz in range(NZ):
        z_copies("wait", tiles + queries, (dz,))

    to_three = (x == 3) | has_extra

    @pl.when(to_three)
    def _():
        arrived(kv_ref.at[c, pl.ds(0, 3 * NZ * CUBE_DEV)], x_send)
        arrived(qf_ref.at[pl.ds(0, 3)], xq_send)

    @pl.when(jnp.logical_not(to_three))
    def _():
        arrived(kv_ref.at[c, pl.ds(0, 2 * NZ * CUBE_DEV)], x_send)
        arrived(qf_ref.at[pl.ds(0, 2)], xq_send)

    for side, t in ((0, 0), (1, 2), (0, 1), (1, 3)):
        total = product(left if side else right, t)
        arrived(passed.at[t], passed_recv.at[t])
        part[2 * side, t] = (total + passed[t].astype(f32)).astype(bf16)
        onward(side, t).start()

    def rows_of(core):
        return pl.ds(pl.multiple_of(core * BAND_CORE, BAND_CORE), BAND_CORE)

    def columns(core, t):
        return pl.ds(pl.multiple_of(core * COLS + t * TILE, TILE), TILE)

    def give(t):
        return remote(
            done.at[t, rows_of(1 - c)], out_ref.at[:, columns(c, t)],
            done_send.at[0], done_recv, here, 2 * y + 1 - c,
        )

    def keep(t):
        return pltpu.make_async_copy(done.at[t, rows_of(c)], out_ref.at[:, columns(c, t)], done_send.at[1])

    band_here(3)
    for t in (2, 0, 3, 1):
        total = product(y, t)
        for side in range(2):
            arrived(landed.at[side, t], landed_recv.at[side, t])
            total = total + landed[side, t].astype(f32)
        done[t] = total.astype(bf16)
        give(t).start()
        keep(t).start()

    arrived(passed, part_send.at[0])
    arrived(landed, part_send.at[1])
    arrived(out_ref.at[:, half(c)], done_send.at[0])
    arrived(out_ref.at[:, half(c)], done_send.at[1])
    arrived(out_ref.at[:, half(1 - c)], done_recv)
    w_away.wait_send()
    arrived(att.at[c], t_send)


def body(query_states, key_states, value_states, gate_states, selection, out_weight):
    bf16 = jnp.bfloat16
    any_spec = pl.BlockSpec(memory_space=pl.ANY)
    dma, vmem = pltpu.SemaphoreType.DMA, pltpu.VMEM
    padded = jnp.pad(selection, ((0, 8 - CUBE_DEV), (0, 128 - TOPK)))
    owner = padded // CUBE_DEV
    places = (owner % NX * NZ + owner // NX) * CUBE_DEV + padded % CUBE_DEV
    cubes = vmem((NX, NZ, CUBE, HEAD_DIM), bf16)
    halves = vmem((NX, NZ, 2, CUBE // 2, HEAD_DIM), bf16)
    return pl.pallas_call(
        kernel,
        out_shape=jax.ShapeDtypeStruct((BAND_CORE, 2 * COLS), bf16),
        in_specs=[any_spec] * 6,
        out_specs=any_spec,
        scratch_shapes=[
            vmem((2, 5 * NZ * CUBE_DEV, CUBE, HEAD_DIM), bf16),
            cubes,
            cubes,
            vmem((NX, NZ, 8, 128), jnp.int32),
            pltpu.SMEM((NX, NZ, 8, 128), jnp.int32),
            vmem((2, N_CUBES, HEAD_DIM), bf16),
            vmem((2, 2 * CUBE, TOPK * CUBE), jnp.float32),
            vmem((2, 2 * CUBE, N_CUBES), jnp.float32),
            halves,
            halves,
            vmem((3, 2, 2, CUBE // 2, FEATS), bf16),
            vmem((2 * CUBE_DEV, CUBE // 2, FEATS), bf16),
            vmem((2, ROWS, FEATS), bf16),
            vmem((2 * FEATS, COLS), bf16),
            vmem((3, TILES, BAND, TILE), bf16),
            vmem((TILES, BAND, TILE), bf16),
            vmem((2, TILES, BAND, TILE), bf16),
            vmem((TILES, BAND, TILE), bf16),
            dma((NZ, 2, 4)), dma((NZ, 4)),
            dma, dma((NZ,)), dma, dma, dma, dma,
            dma, dma, dma, dma, dma,
            dma, dma((NZ,)), dma((NZ, 2)), dma, dma, dma((3,)), dma, dma((NY,)),
            dma((2,)), dma((TILES,)), dma((2, TILES)), dma((2,)), dma,
        ],
        compiler_params=pltpu.CompilerParams(
            collective_id=0, has_side_effects=True, vmem_limit_bytes=60 * 2**20
        ),
        name="sparse_attention",
    )(
        places,
        query_states.reshape(3, 2, CUBE, FEATS),
        key_states.reshape(CUBE_DEV, CUBE, FEATS),
        value_states.reshape(CUBE_DEV, CUBE, FEATS),
        gate_states.reshape(2 * CUBE_DEV, CUBE // 2, FEATS),
        out_weight,
    )


def solution(mesh):
    placed = (
        P("seq", "head"),
        P("seq", "head"),
        P("seq", "head"),
        P("seq", "head"),
        P("seq", None),
        P("head", None),
    )
    return jax.shard_map(
        body, mesh=mesh, in_specs=placed, out_specs=P(("seq", "head"), None), check_vma=False
    )
```

```python
import functools
import math

import jax
import jax.numpy as jnp
from jax import lax
from jax.experimental import pallas as pl
from jax.experimental.pallas import tpu as pltpu
from jax.sharding import PartitionSpec as P

MESH = pl.DeviceIdType.MESH
HEAD_DIM = 128
CUBE = 64
CUBE_DEV = 6
TOPK = 32
NZ, NX = 8, 4
ROWS = CUBE * CUBE_DEV
HEADS_DEV = 5
NY = 4
ORDER = (0, 1, 7, 2, 6, 3, 5, 4)
XORDER = (1, 3, 2)
FEATS = HEADS_DEV * HEAD_DIM
BAND = ROWS // NY
BAND_CORE = BAND // 2
COLS = 2560
TILE = 640
TILES = COLS // TILE
N_CUBES = NZ * NX * CUBE_DEV
GROUP = 4
WIDTH = GROUP * CUBE
LAG = 4
ROUNDS = ((0,), (1, 7), (2, 6), (3, 5), (4,))
CONTRACT_LAST = (((1,), (1,)), ((), ()))
EXP_SCALE = HEAD_DIM ** (-0.5) * math.log2(math.e)


def place():
    seq, head = lax.axis_index("seq"), lax.axis_index("head")
    return seq // NX, seq % NX, head // 2, head % 2


def remote(src, dst, send_sem, recv_sem, seq, head):
    return pltpu.make_async_remote_copy(
        src_ref=src,
        dst_ref=dst,
        send_sem=send_sem,
        recv_sem=recv_sem,
        device_id={"seq": seq, "head": head},
        device_id_type=MESH,
    )


def arrived(ref, sem):
    pltpu.make_async_copy(ref, ref, sem).wait()


def greet(z, x, y, c):
    barrier = pltpu.get_barrier_semaphore()
    for dz in range(NZ):
        for dc in range(2):
            if dz or dc:
                pl.semaphore_signal(
                    barrier,
                    inc=1,
                    device_id={"seq": (z + dz) % NZ * NX + x, "head": 2 * y + (c + dc) % 2},
                    device_id_type=MESH,
                )
    for dx in range(1, NX):
        pl.semaphore_signal(
            barrier,
            inc=1,
            device_id={"seq": z * NX + (x + dx) % NX, "head": 2 * y + c},
            device_id_type=MESH,
        )
    for dy in (1, 3):
        pl.semaphore_signal(
            barrier,
            inc=1,
            device_id={"seq": z * NX + x, "head": 2 * ((y + dy) % NY) + c},
            device_id_type=MESH,
        )
    pl.semaphore_wait(barrier, 2 * NZ - 1 + NX - 1 + 2)


def kernel(
    sel_ref, q_ref, k_ref, v_ref, gate_hbm, w_ref, out_ref,
    kv_ref, qr_ref, qf_ref, all_sel_ref, sel, pooled, scores, coarse_scores, o_ref,
    relay_ref, a_ref, gate_ref, att, weight, part, passed, landed, done,
    z_send, z_recv, x_send, x_recv, xq_send, xq_recv, c_send, c_recv,
    sz_send, sz_recv, sx_send, sx_recv, pick_sem,
    o_send, o_recv, r_send, r_recv, gate_sem, w_sem, t_send, t_recv,
    part_send, passed_recv, landed_recv, done_send, done_recv,
):
    f32, bf16 = jnp.float32, jnp.bfloat16
    z, x, y, c = place()
    here = z * NX + x
    sibling = 2 * y + 1 - c
    main_slot = x + x // 3
    extra_slot = 4 - x // 3
    has_extra = z % 4 != 3
    member = (x != 3) | has_extra
    greet(z, x, y, c)

    def tile_at(which, slot, zs):
        return kv_ref.at[which, pl.ds((slot * NZ + zs) * CUBE_DEV, CUBE_DEV)]

    def half(core):
        return pl.ds(pl.multiple_of(core * COLS, COLS), COLS)

    def block(core):
        return pl.ds(pl.multiple_of(core * FEATS, FEATS), FEATS)

    w_own = pltpu.make_async_copy(w_ref.at[:, half(c)], weight.at[block(c)], w_sem.at[0])
    w_away = remote(w_ref.at[:, half(1 - c)], weight.at[block(c)], w_sem.at[1], w_sem.at[2], here, sibling)

    def sel_z(n, dz):
        return remote(
            sel_ref, all_sel_ref.at[x, z], sz_send, sz_recv, (z + dz) % NZ * NX + x, 2 * y + c
        )

    def sel_x(dx):
        return remote(
            all_sel_ref.at[x], all_sel_ref.at[x], sx_send, sx_recv, z * NX + (x + dx) % NX, 2 * y + c
        )

    pltpu.make_async_copy(sel_ref, all_sel_ref.at[x, z], sz_recv).start()
    for n, dz in enumerate(ORDER):
        if dz:
            sel_z(n, dz).start()

    def z_copies(act, kinds, dzs):
        for dz in dzs:
            zt = (z + dz) % NZ
            for cc in range(2):
                source = k_ref if cc == 0 else v_ref

                def one(cond, kind, src, dst):
                    def away():
                        copy = remote(
                            src, dst, z_send.at[dz, cc, kind], z_recv.at[z, kind], zt * NX + x, 2 * y + cc
                        )
                        if act == "start":
                            copy.start()
                        else:
                            copy.wait_send()

                    if dz:
                        pl.when(cond)(away)
                    else:
                        pl.when(cond & (c != cc))(away)
                        if act == "start":
                            pl.when(cond & (c == cc))(
                                lambda: pltpu.make_async_copy(src, dst, z_recv.at[z, kind]).start()
                            )

                is_main = c == zt // 5
                col = pl.ds(pl.multiple_of(zt % 5 * HEAD_DIM, HEAD_DIM), HEAD_DIM)
                is_extra = (c == 1) & (zt % 4 != 3)
                xcol = pl.ds(pl.multiple_of((3 + zt // 4) * HEAD_DIM, HEAD_DIM), HEAD_DIM)
                rank = zt % 4 - zt % 4 // 3
                if 0 in kinds:
                    one(is_main, 0, source.at[:, :, col], tile_at(cc, main_slot, z))
                    one(is_extra, 1, source.at[:, :, xcol], tile_at(cc, extra_slot, z))
                if 2 in kinds:
                    one(is_main, 2, q_ref.at[:, cc, :, col], qr_ref.at[pl.ds(0, 3), z])
                    one(is_extra, 3, q_ref.at[rank, cc, :, xcol], qr_ref.at[3, z])

    tiles, queries = (0, 1), (2, 3)
    for r in range(2):
        z_copies("start", tiles, ROUNDS[r])
    w_own.start()
    gate_in = pltpu.make_async_copy(gate_hbm, gate_ref, gate_sem)
    gate_in.start()
    def x_copies(dz, act, kind):
        zs = (z + dz) % NZ
        for dx in XORDER:
            xt = (x + dx) % NX
            slot = main_slot if kind == 0 else 4

            def away():
                copy = remote(
                    tile_at(c, slot, zs), tile_at(c, x, zs),
                    x_send, x_recv.at[zs], z * NX + xt, 2 * y + c,
                )
                if act == "start":
                    copy.start()
                else:
                    copy.wait_send()

            pl.when(xt != 3 if kind == 0 else (xt == 3) & has_extra)(away)

    def core_copy(xs, zs):
        return remote(
            tile_at(c, xs, zs), tile_at(c, xs, zs),
            c_send, c_recv, here, sibling,
        )

    def take_x(zs):
        pl.when(member)(lambda: arrived(kv_ref.at[c, pl.ds(0, 3 * CUBE_DEV)], x_recv.at[zs]))
        for dx in XORDER:
            xs = (x + dx) % NX

            @pl.when(member)
            def _():
                core_copy(xs, zs).start()

    for r, dzs in enumerate(ROUNDS):
        for dz in dzs:
            zs = (z + dz) % NZ
            arrived(tile_at(c, main_slot, zs), z_recv.at[zs, 0])
            x_copies(dz, "start", 0)
            pl.when(x != 3)(lambda: core_copy(x, zs).start())
        if r == 1:
            z_copies("start", tiles, ROUNDS[2])
        if r == 3:
            z_copies("start", tiles, ROUNDS[4])
        if r == 2:
            z_copies("start", tiles, ROUNDS[3])
            for n in range(3):
                z_copies("start", queries, ROUNDS[n])
        if r == 3:
            for n in range(3, 5):
                z_copies("start", queries, ROUNDS[n])
        for dz in dzs:
            zs = (z + dz) % NZ
            pl.when(has_extra)(lambda: arrived(tile_at(c, extra_slot, zs), z_recv.at[zs, 1]))
            x_copies(dz, "start", 1)
            pl.when((x == 3) & has_extra)(lambda: core_copy(x, zs).start())
        if r == 2:
            arrived(all_sel_ref.at[x], sz_recv)
            for dx in range(1, NX):
                sel_x(dx).start()
        if r:
            for dz in ROUNDS[r - 1]:
                take_x((z + dz) % NZ)

    def xq_copies(dz, act):
        zs = (z + dz) % NZ
        for dx in range(NX):
            xt = (x + dx) % NX

            def away():
                src, dst = qr_ref.at[xt, zs], qf_ref.at[x, zs]
                if dx:
                    copy = remote(src, dst, xq_send, xq_recv, z * NX + xt, 2 * y + c)
                    if act == "start":
                        copy.start()
                    else:
                        copy.wait_send()
                elif act == "start":
                    pltpu.make_async_copy(src, dst, xq_recv).start()

            pl.when((xt != 3) | has_extra)(away)

    arrived(all_sel_ref.at[pl.ds(0, NX - 1)], sx_recv)
    picks = pltpu.make_async_copy(all_sel_ref, sel, pick_sem)
    picks.start()

    for r, dzs in enumerate(ROUNDS):
        for dz in dzs:
            zs = (z + dz) % NZ
            arrived(qr_ref.at[pl.ds(0, 3), zs], z_recv.at[zs, 2])
            pl.when(has_extra)(lambda: arrived(qr_ref.at[3, zs], z_recv.at[zs, 3]))
            xq_copies(dz, "start")
    for dz in ROUNDS[-1]:
        take_x((z + dz) % NZ)
    w_away.start()

    def pool(which):
        def some(i, _):
            sums = jnp.sum(kv_ref[which, pl.ds(i * 16, 16)].astype(f32), axis=1)
            pooled[which, pl.ds(pl.multiple_of(i * 16, 16), 16), :] = (sums * (1.0 / CUBE)).astype(bf16)
            return 0

        lax.fori_loop(0, N_CUBES // 16, some, 0)

    pool(c)

    @pl.when(member)
    def _():
        arrived(qf_ref, xq_recv)
        arrived(kv_ref.at[1 - c, pl.ds(0, N_CUBES)], c_recv)

    pool(1 - c)
    picks.wait()

    rank = x + x // 3 * (z % 4 - x)
    cube = rank * 2 + c - rank // 3 * 2

    def target(n):
        return (z + 4 + (1 - n % 2 * 2) * ((n + 1) // 2)) % NZ

    def rows(which, xs, zs, g):
        tiles = [
            kv_ref[which, sel[xs, zs, cube, g * GROUP + n]]
            for n in range(GROUP)
        ]
        return jnp.concatenate(tiles, axis=0)

    def pair_rows(which, pair, zs, g):
        return jnp.concatenate([rows(which, 2 * pair, zs, g), rows(which, 2 * pair + 1, zs, g)], axis=1)

    def blend(pair, zs, top, pair_ahead, zs_ahead):
        acc = [jnp.zeros((CUBE, HEAD_DIM), f32) for _ in range(2)]
        total = jnp.zeros((2 * CUBE, 128), f32)
        peak = None
        if top is not None:
            e = jnp.exp2((coarse_scores[pair] - top[1]) * EXP_SCALE)
            coarse = jnp.dot(e.astype(bf16), pooled[1], preferred_element_type=f32)
            coarse = coarse / jnp.sum(e, axis=1, keepdims=True)
        q = [qf_ref[2 * pair_ahead + n, zs_ahead] for n in range(2)]
        s = lax.dot_general(jnp.concatenate(q, axis=0), pooled[0], CONTRACT_LAST, preferred_element_type=f32)
        coarse_scores[pair_ahead] = s
        coarse_peak = jnp.max(s, axis=1, keepdims=True)
        zero = jnp.zeros((CUBE, HEAD_DIM), bf16)
        ahead = jnp.concatenate([
            jnp.concatenate([q[0], zero], axis=1),
            jnp.concatenate([zero, q[1]], axis=1),
        ], axis=0)
        for g in range(TOPK // GROUP):
            cols = slice(g * WIDTH, (g + 1) * WIDTH)
            s = lax.dot_general(ahead, pair_rows(0, pair_ahead, zs_ahead, g), CONTRACT_LAST, preferred_element_type=f32)
            scores[pair_ahead, :, cols] = s
            part_peak = jnp.maximum(s[:, :128], s[:, 128:])
            peak = part_peak if peak is None else jnp.maximum(peak, part_peak)
            if top is not None:
                e = jnp.exp2((scores[pair, :, cols] - top[0]) * EXP_SCALE)
                total = total + (e[:, :128] + e[:, 128:])
                out = jnp.dot(e.astype(bf16), pair_rows(1, pair, zs, g), preferred_element_type=f32)
                acc = [acc[0] + out[:CUBE, :HEAD_DIM], acc[1] + out[CUBE:, HEAD_DIM:]]
        if top is not None:
            mixed = jnp.concatenate(acc, axis=0) / jnp.sum(total, axis=1, keepdims=True) + coarse
            for n in range(2):
                o_ref[2 * pair + n, zs] = mixed[n * CUBE:(n + 1) * CUBE].astype(bf16).reshape(2, CUBE // 2, HEAD_DIM)
        return jnp.max(peak, axis=1, keepdims=True), coarse_peak

    def o_copy(dx, n, zs):
        xt = (x + dx) % NX
        return remote(
            o_ref.at[xt, zs], relay_ref.at[x, zs], o_send, o_recv.at[zs], z * NX + xt, 2 * y + c
        )

    def pass_copies(n, zs, act):
        def one(cond, kind, core, src, dst):
            def away():
                copy = remote(src, dst, r_send.at[n, kind], r_recv, zs * NX + x, 2 * y + core)
                if act == "start":
                    copy.start()
                else:
                    copy.wait_send()

            stays = (zs == z) & (c == core)
            pl.when(cond & jnp.logical_not(stays))(away)
            if act == "start":
                pl.when(cond & stays)(
                    lambda: pltpu.make_async_copy(src, dst, r_recv).start()
                )

        col = pl.ds(pl.multiple_of(z % 5 * HEAD_DIM, HEAD_DIM), HEAD_DIM)
        one(z >= 0, 0, z // 5, relay_ref.at[pl.ds(0, 3), zs], a_ref.at[:, c, :, :, col])
        xcol = pl.ds(pl.multiple_of((3 + z // 4) * HEAD_DIM, HEAD_DIM), HEAD_DIM)
        third = z % 4 - z % 4 // 3
        one(has_extra, 1, 1, relay_ref.at[3, zs], a_ref.at[third, c, :, :, xcol])

    def pass_on(n):
        zs = target(n)
        pl.when(has_extra)(lambda: arrived(relay_ref.at[:, zs], o_recv.at[zs]))
        pl.when(jnp.logical_not(has_extra))(lambda: arrived(relay_ref.at[pl.ds(0, 3), zs], o_recv.at[zs]))
        pass_copies(n, zs, "start")

    def step(n, top):
        zs = target(n)
        top = blend(0, zs, top, 1, zs)
        top = blend(1, zs, top, 0, target(jnp.minimum(n + 1, NZ - 1)))

        @pl.when(member)
        def _():
            pltpu.make_async_copy(o_ref.at[x, zs], relay_ref.at[x, zs], o_recv.at[zs]).start()
            for dx in XORDER:
                o_copy(dx, n, zs).start()

        pl.when(n >= LAG)(lambda: pass_on(n - LAG))
        return top

    lax.fori_loop(0, NZ, step, blend(None, None, None, 0, target(0)))
    for n in range(NZ - LAG, NZ):
        pass_on(n)

    gate_in.wait()
    arrived(a_ref, r_recv)

    def band_rows(band):
        return pl.ds(pl.multiple_of(band * BAND, BAND), BAND)

    def att_away(n, band):
        return remote(
            att.at[c, band_rows(band)], att.at[c, band_rows(band)], t_send, t_recv.at[n], here, sibling
        )

    bands = [(y + dy) % NY for dy in (2, 1, 3, 0)]
    for n, band in enumerate(bands):
        for piece in range(3):
            part_of = band * 3 + piece
            mixed = a_ref[part_of // 4, part_of // 2 % 2, part_of % 2].astype(f32)
            gates = jax.nn.sigmoid(gate_ref[part_of].astype(f32))
            start = pl.multiple_of(part_of * (CUBE // 2), CUBE // 2)
            att[c, pl.ds(start, CUBE // 2), :] = (gates * mixed).astype(bf16)
        att_away(n, band).start()
    w_own.wait()
    arrived(weight.at[block(1 - c)], w_sem.at[2])

    def band_here(n):
        arrived(att.at[1 - c, band_rows(bands[n])], t_recv.at[n])

    def product(band, t):
        rows = band_rows(band)
        cols = slice(t * TILE, (t + 1) * TILE)
        total = jnp.dot(att[0, rows, :], weight[:FEATS, cols], preferred_element_type=f32)
        return total + jnp.dot(att[1, rows, :], weight[FEATS:, cols], preferred_element_type=f32)

    right, left = (y + 1) % NY, (y + 3) % NY

    def across(t):
        return remote(
            part.at[1, t], passed.at[t], part_send.at[0], passed_recv.at[t],
            here, 2 * (right if t < 2 else left) + c,
        )

    def onward(side, t):
        return remote(
            part.at[2 * side, t], landed.at[side, t], part_send.at[1], landed_recv.at[side, t],
            here, 2 * (left if side else right) + c,
        )

    band_here(0)
    for t in (0, 2, 1, 3):
        part[1, t] = product((y + 2) % NY, t).astype(bf16)
        across(t).start()
    band_here(1)
    band_here(2)
    for side, t in ((0, 2), (1, 0), (0, 3), (1, 1)):
        part[2 * side, t] = product(left if side else right, t).astype(bf16)
        onward(side, t).start()
    @pl.when(member)
    def _():
        arrived(o_ref.at[pl.ds(0, 3)], o_send)
        arrived(kv_ref.at[c, pl.ds(0, N_CUBES)], c_send)

    for n in range(NZ):
        pass_copies(n, target(n), "wait")
    arrived(all_sel_ref.at[pl.ds(0, NX - 1)], sx_send)
    arrived(all_sel_ref.at[x, pl.ds(0, NZ - 1)], sz_send)
    for dz in range(NZ):
        z_copies("wait", tiles + queries, (dz,))

    to_three = (x == 3) | has_extra

    @pl.when(to_three)
    def _():
        arrived(kv_ref.at[c, pl.ds(0, 3 * NZ * CUBE_DEV)], x_send)
        arrived(qf_ref.at[pl.ds(0, 3)], xq_send)

    @pl.when(jnp.logical_not(to_three))
    def _():
        arrived(kv_ref.at[c, pl.ds(0, 2 * NZ * CUBE_DEV)], x_send)
        arrived(qf_ref.at[pl.ds(0, 2)], xq_send)

    for side, t in ((0, 0), (1, 2), (0, 1), (1, 3)):
        total = product(left if side else right, t)
        arrived(passed.at[t], passed_recv.at[t])
        part[2 * side, t] = (total + passed[t].astype(f32)).astype(bf16)
        onward(side, t).start()

    def rows_of(core):
        return pl.ds(pl.multiple_of(core * BAND_CORE, BAND_CORE), BAND_CORE)

    def columns(core, t):
        return pl.ds(pl.multiple_of(core * COLS + t * TILE, TILE), TILE)

    def give(t):
        return remote(
            done.at[t, rows_of(1 - c)], out_ref.at[:, columns(c, t)],
            done_send.at[0], done_recv, here, 2 * y + 1 - c,
        )

    def keep(t):
        return pltpu.make_async_copy(done.at[t, rows_of(c)], out_ref.at[:, columns(c, t)], done_send.at[1])

    band_here(3)
    for t in (2, 0, 3, 1):
        total = product(y, t)
        for side in range(2):
            arrived(landed.at[side, t], landed_recv.at[side, t])
            total = total + landed[side, t].astype(f32)
        done[t] = total.astype(bf16)
        give(t).start()
        keep(t).start()

    arrived(passed, part_send.at[0])
    arrived(landed, part_send.at[1])
    arrived(out_ref.at[:, half(c)], done_send.at[0])
    arrived(out_ref.at[:, half(c)], done_send.at[1])
    arrived(out_ref.at[:, half(1 - c)], done_recv)
    w_away.wait_send()
    arrived(att.at[c], t_send)


def body(query_states, key_states, value_states, gate_states, selection, out_weight):
    bf16 = jnp.bfloat16
    any_spec = pl.BlockSpec(memory_space=pl.ANY)
    dma, vmem = pltpu.SemaphoreType.DMA, pltpu.VMEM
    padded = jnp.pad(selection, ((0, 8 - CUBE_DEV), (0, 128 - TOPK)))
    owner = padded // CUBE_DEV
    places = (owner % NX * NZ + owner // NX) * CUBE_DEV + padded % CUBE_DEV
    cubes = vmem((NX, NZ, CUBE, HEAD_DIM), bf16)
    halves = vmem((NX, NZ, 2, CUBE // 2, HEAD_DIM), bf16)
    return pl.pallas_call(
        kernel,
        out_shape=jax.ShapeDtypeStruct((BAND_CORE, 2 * COLS), bf16),
        in_specs=[any_spec] * 6,
        out_specs=any_spec,
        scratch_shapes=[
            vmem((2, 5 * NZ * CUBE_DEV, CUBE, HEAD_DIM), bf16),
            cubes,
            cubes,
            vmem((NX, NZ, 8, 128), jnp.int32),
            pltpu.SMEM((NX, NZ, 8, 128), jnp.int32),
            vmem((2, N_CUBES, HEAD_DIM), bf16),
            vmem((2, 2 * CUBE, TOPK * CUBE), jnp.float32),
            vmem((2, 2 * CUBE, N_CUBES), jnp.float32),
            halves,
            halves,
            vmem((3, 2, 2, CUBE // 2, FEATS), bf16),
            vmem((2 * CUBE_DEV, CUBE // 2, FEATS), bf16),
            vmem((2, ROWS, FEATS), bf16),
            vmem((2 * FEATS, COLS), bf16),
            vmem((3, TILES, BAND, TILE), bf16),
            vmem((TILES, BAND, TILE), bf16),
            vmem((2, TILES, BAND, TILE), bf16),
            vmem((TILES, BAND, TILE), bf16),
            dma((NZ, 2, 4)), dma((NZ, 4)),
            dma, dma((NZ,)), dma, dma, dma, dma,
            dma, dma, dma, dma, dma,
            dma, dma((NZ,)), dma((NZ, 2)), dma, dma, dma((3,)), dma, dma((NY,)),
            dma((2,)), dma((TILES,)), dma((2, TILES)), dma((2,)), dma,
        ],
        compiler_params=pltpu.CompilerParams(
            collective_id=0, has_side_effects=True, vmem_limit_bytes=60 * 2**20
        ),
        name="sparse_attention",
    )(
        places,
        query_states.reshape(3, 2, CUBE, FEATS),
        key_states.reshape(CUBE_DEV, CUBE, FEATS),
        value_states.reshape(CUBE_DEV, CUBE, FEATS),
        gate_states.reshape(2 * CUBE_DEV, CUBE // 2, FEATS),
        out_weight,
    )


def solution(mesh):
    placed = (
        P("seq", "head"),
        P("seq", "head"),
        P("seq", "head"),
        P("seq", "head"),
        P("seq", None),
        P("head", None),
    )
    return jax.shard_map(
        body, mesh=mesh, in_specs=placed, out_specs=P(("seq", "head"), None), check_vma=False
    )
```
